128 devices in a mesh: seq: 16 (over y, x_lo, core), tp: 8 (over z, x_hi).
Axes of the slice: x: 4 (x_hi: 2, x_lo: 2; x = x_hi * 2 + x_lo), y: 4, z: 4, core: 2. Of those that a mesh axis runs over, the one named last changes fastest.
Arguments:
- grad_out: bfloat16 [32768, 8192], P('seq', 'tp'), may hold values from -6 to 6
- select: int32 [4096], P('seq'), may hold values from 0 to 2047, as said below
- router: float32 [4096], P('seq'), may hold values from 0.1 to 1
- query: bfloat16 [4096, 8192], P('seq', 'tp'), may hold values from -7 to 7
- key_rows: bfloat16 [4096, 1024], P('seq', 'tp'), may hold values from -6 to 6
- value_rows: bfloat16 [4096, 1024], P('seq', 'tp'), may hold values from -6 to 6
- out_weight: bfloat16 [8192, 8192], P('tp'), may hold values from -0.0625 to 0.0625
Outputs:
- grad_query: bfloat16 [4096, 8192], P('seq', 'tp')
- grad_key: bfloat16 [4096, 1024], P('seq', 'tp')
- grad_value: bfloat16 [4096, 1024], P('seq', 'tp')
- grad_router: float32 [4096], P('seq')
The draws below stay inside these ranges and needn't reach their ends.
Inputs may be any that keep to these rules, and one draw needn't show every extreme that they name: `select`: within each aligned block of 256 rows (one sequence shard) the positions are distinct and increasing, and every block holds its shard's first and last token.
All inputs are finite; a program needn't handle non-finite values.
Results may differ from the reference program's by a relative error of at most 0.008.
Values may be sent and summed in bfloat16 or wider, within the bound.
A program may use at most 192 MiB of HBM per device.

```python
import math
import jax
import jax.numpy as jnp
from jax import lax

D = 8192
HEADS = 64
KV_HEADS = 8
HD = 128
TOK_DEV = 2048
SEL_DEV = 256
TOKENS = 32768
SELECTED = 4096


def draw_select(key, part):
    key = jax.random.fold_in(key, 11)
    shard_keys = jax.random.split(key, SELECTED // SEL_DEV)

    def one_shard(shard_key):
        middle = jax.random.permutation(shard_key, TOK_DEV - 2)[:SEL_DEV - 2] + 1
        middle = jnp.sort(middle).astype(jnp.int32)
        first = jnp.zeros((1,), jnp.int32)
        final = jnp.full((1,), TOK_DEV - 1, jnp.int32)
        return jnp.concatenate([first, middle, final])
    return jax.vmap(one_shard)(shard_keys).reshape(SELECTED).astype(jnp.int32)


def draw_query(key, part):
    key = jax.random.fold_in(key, 21)
    drawn = jnp.clip(1.5 * jax.random.normal(key, (SELECTED, HEADS * HD), jnp.float32), -6.0, 6.0)
    return drawn.astype(jnp.bfloat16)


def draw_key_rows(key, part):
    key = jax.random.fold_in(key, 31)
    drawn = jnp.clip(1.5 * jax.random.normal(key, (SELECTED, KV_HEADS * HD), jnp.float32), -6.0, 6.0)
    return drawn.astype(jnp.bfloat16)


def block_levels(own_key, shape, cuts, smallest, high):
    gain, own = 1.0, jax.random.fold_in(own_key, 6)
    for dim, parts in cuts:
        heights = jnp.exp(jax.random.uniform(jax.random.fold_in(own, dim), (parts,), jnp.float32, smallest / len(cuts), high / len(cuts)))
        gain = gain * jnp.repeat(heights, shape[dim] // parts).reshape([-1 if axis == dim else 1 for axis in range(len(shape))])
    return gain


def bell_draw(own_key, dims, width, limit, cuts=(), kind=jnp.bfloat16):
    values = width * jax.random.normal(own_key, dims, jnp.float32)
    if cuts:
        values = values * block_levels(own_key, dims, cuts, -0.22, 0.18)
    return jnp.clip(values, -limit, limit).astype(kind)


def setup_inputs(seed: int = 0) -> dict:
    streams_of = jax.random.split(jax.random.key(seed), 8)
    return {
        "grad_out": bell_draw(streams_of[0], (TOKENS, D), 1.0, 6.0, ((0, 16), (1, 8))),
        "select": draw_select(jax.random.fold_in(streams_of[7], 71), 0),
        "router": jnp.clip(jnp.exp(math.log(1.0) - 2.3025851 * jax.random.uniform(streams_of[2], (SELECTED,), jnp.float32) ** block_levels(streams_of[2], (SELECTED,), ((0, 16),), -0.2, 0.2)), 0.1, 1.0),
        "query": draw_query(jax.random.fold_in(streams_of[7], 71), 0),
        "key_rows": draw_key_rows(jax.random.fold_in(streams_of[7], 71), 0),
        "value_rows": bell_draw(streams_of[5], (SELECTED, KV_HEADS * HD), 1.0, 6.0, ((0, 16), (1, 8))),
        "out_weight": bell_draw(streams_of[6], (HEADS * HD, D), (HEADS * HD) ** -0.5, 0.0625, ((0, 8),)),
    }


def reference(grad_out, select, router, query, key_rows, value_rows, out_weight):
    factor = 1.0 / math.sqrt(HD)
    group = HEADS // KV_HEADS
    shard_index = jnp.arange(SELECTED, dtype=jnp.int32) // SEL_DEV
    places = (shard_index * TOK_DEV + select).astype(jnp.int32)
    picked = jnp.take(grad_out, places, axis=0)
    allowed = places[None, :] <= places[:, None]
    query_heads = query.reshape(SELECTED, HEADS, HD).transpose(1, 0, 2)
    key_heads = jnp.repeat(key_rows.reshape(SELECTED, KV_HEADS, HD).transpose(1, 0, 2), group, axis=0)
    value_heads = jnp.repeat(value_rows.reshape(SELECTED, KV_HEADS, HD).transpose(1, 0, 2), group, axis=0)

    def forward_head(operands):
        queries, key_block, values = operands
        scores = jnp.dot(queries, key_block.T, preferred_element_type=jnp.float32) * factor
        scores = jnp.where(allowed, scores, -jnp.inf)
        row_top = lax.optimization_barrier(jnp.max(scores, axis=1, keepdims=True))
        log_total = row_top + jnp.log(lax.optimization_barrier(jnp.sum(jnp.exp(scores - row_top), axis=1, keepdims=True)))
        weights = jnp.exp(scores - log_total).astype(jnp.bfloat16)
        attended = jnp.dot(weights, values, preferred_element_type=jnp.float32).astype(jnp.bfloat16)
        return (attended, log_total[:, 0])
    attended_heads, log_totals = lax.map(forward_head, (query_heads, key_heads, value_heads))
    attended = attended_heads.transpose(1, 0, 2).reshape(SELECTED, HEADS * HD)
    block = jnp.dot(attended, out_weight, preferred_element_type=jnp.float32)
    grad_router = lax.optimization_barrier(jnp.sum(picked.astype(jnp.float32) * block, axis=1))
    grad_block = (router[:, None] * picked.astype(jnp.float32)).astype(jnp.bfloat16)
    grad_attended = jnp.dot(grad_block, out_weight.T, preferred_element_type=jnp.float32).astype(jnp.bfloat16)
    grad_heads = grad_attended.reshape(SELECTED, HEADS, HD).transpose(1, 0, 2)
    deltas = lax.optimization_barrier(jnp.sum(grad_heads.astype(jnp.float32) * attended_heads.astype(jnp.float32), axis=2))

    def backward_head(operands):
        queries, key_block, values, gradients, log_total, delta_row = operands
        scores = jnp.dot(queries, key_block.T, preferred_element_type=jnp.float32) * factor
        probs = jnp.where(allowed, jnp.exp(scores - log_total[:, None]), 0.0)
        grad_probs = jnp.dot(gradients, values.T, preferred_element_type=jnp.float32)
        grad_scores = (probs * (grad_probs - delta_row[:, None])).astype(jnp.bfloat16)
        grad_values = jnp.dot(probs.astype(jnp.bfloat16).T, gradients, preferred_element_type=jnp.float32)
        grad_keys = jnp.dot(grad_scores.T, queries, preferred_element_type=jnp.float32) * factor
        grad_queries = (jnp.dot(grad_scores, key_block, preferred_element_type=jnp.float32) * factor).astype(jnp.bfloat16)
        return (grad_queries, grad_keys, grad_values)
    grad_q, grad_k, grad_v = lax.map(backward_head, (query_heads, key_heads, value_heads, grad_heads, log_totals, deltas))
    grad_k = lax.optimization_barrier(jnp.sum(grad_k.reshape(KV_HEADS, group, SELECTED, HD), axis=1)).astype(jnp.bfloat16)
    grad_v = lax.optimization_barrier(jnp.sum(grad_v.reshape(KV_HEADS, group, SELECTED, HD), axis=1)).astype(jnp.bfloat16)

    def flatten(stacked):
        return stacked.transpose(1, 0, 2).reshape(SELECTED, stacked.shape[0] * HD)
    return (flatten(grad_q), flatten(grad_k), flatten(grad_v), grad_router)
```

```python
import math

import jax
import jax.numpy as jnp
from jax import lax
from jax.experimental import pallas as pl
from jax.experimental.pallas import tpu as pltpu
from jax.sharding import PartitionSpec as P

F32 = jnp.float32
BF = jnp.bfloat16
MESH = pl.DeviceIdType.MESH
NN = ((1,), (0,))
NT = ((1,), (1,))
TN = ((0,), (0,))

HD = 128
GROUP = 8
SEQ = 16
TP = 8
CHIPS = 8
ROWS = 256
HALF = 128
LANES = 1024
WIDE = 1024
FACTOR = 1.0 / math.sqrt(HD)
SCALE = FACTOR * math.log2(math.e)
FLOOR = -1e30


def dot(a, b, dims):
    return lax.dot_general(a, b, (dims, ((), ())), preferred_element_type=F32)


def loop(count, step):
    def run(i, carry):
        step(i)
        return carry

    lax.fori_loop(0, count, run, 0)


def kernel(
    go_hbm,
    w_hbm,
    sel_ref,
    router_ref,
    q_ref,
    k_ref,
    v_ref,
    dq_ref,
    dk_ref,
    dv_ref,
    gr_ref,
    probs,
    w_ref,
    picked,
    kv,
    acc,
    out_part,
    in_part,
    q_t,
    q_s,
    top,
    o_t,
    g_t,
    do_t,
    do_s,
    delta,
    dq_t,
    router_part,
    local_sem,
    kv_send,
    kv_recv,
    side_send,
    pick_send,
    pick_recv,
    part_send,
    part_recv,
    router_send,
    router_recv,
):
    s = lax.axis_index("seq")
    t = lax.axis_index("tp")
    chip = s // 2
    core = s % 2
    z = t // 2
    h = t % 2
    sibling = s + 1 - 2 * core
    z_up = ((z + 1) % 4) * 2 + h
    z_down = ((z + 3) % 4) * 2 + h
    z_far = ((z + 2) % 4) * 2 + h
    x_far = z * 2 + 1 - h
    other = 1 - 2 * h

    go_copies = []
    for p in range(4):
        go_copies.append(
            pltpu.make_async_copy(
                go_hbm.at[pl.ds(p * 512, 512), :],
                probs.at[p // 2, :, pl.ds((p % 2) * WIDE, WIDE)],
                local_sem.at[p],
            )
        )
    for copy in go_copies:
        copy.start()
    w_copy = pltpu.make_async_copy(w_hbm, w_ref, local_sem.at[4])
    w_copy.start()

    barrier = pltpu.get_barrier_semaphore()
    for step in range(1, SEQ):
        pl.semaphore_signal(
            barrier, inc=1, device_id=((s + step) % SEQ, t), device_id_type=MESH
        )
    for step in range(1, TP):
        pl.semaphore_signal(
            barrier, inc=1, device_id=(s, (t + step) % TP), device_id_type=MESH
        )
    kv[s, 0] = k_ref[...]
    kv[s, 1] = v_ref[...]
    pl.semaphore_wait(barrier, SEQ - 1 + TP - 1)

    def kv_copy(step):
        return pltpu.make_async_remote_copy(
            src_ref=kv.at[s],
            dst_ref=kv.at[s],
            send_sem=kv_send.at[step],
            recv_sem=kv_recv.at[s],
            device_id=(((chip + step) % CHIPS) * 2 + core, t),
            device_id_type=MESH,
        )

    def side_copy(step):
        block = ((chip + CHIPS - step) % CHIPS) * 2 + core
        return pltpu.make_async_remote_copy(
            src_ref=kv.at[block],
            dst_ref=kv.at[block],
            send_sem=side_send.at[step],
            recv_sem=kv_recv.at[block],
            device_id=(sibling, t),
            device_id_type=MESH,
        )

    def kv_arrived(block):
        pltpu.make_async_remote_copy(
            src_ref=kv.at[block],
            dst_ref=kv.at[block],
            send_sem=kv_send.at[0],
            recv_sem=kv_recv.at[block],
            device_id=(sibling, t),
            device_id_type=MESH,
        ).wait_recv()

    side_copy(0).start()
    for step in range(1, CHIPS):
        kv_copy(step).start()

    def pick_copy(c, n, slot, to, rows=None):
        src = picked.at[c, slot]
        if rows is not None:
            src = picked.at[c, slot, pl.ds(rows, HALF // 2), :]
        return pltpu.make_async_remote_copy(
            src_ref=src,
            dst_ref=src,
            send_sem=pick_send.at[c, n],
            recv_sem=pick_recv.at[c, n],
            device_id=(s, to),
            device_id_type=MESH,
        )

    def own_sends(c):
        return [
            pick_copy(c, 0, t, z_up),
            pick_copy(c, 1, t, z_down),
            pick_copy(c, 2, t, x_far),
        ]

    def near_sends(c):
        return [
            pick_copy(c, 3, z_down, z_up, 0),
            pick_copy(c, 4, z_up, z_down, HALF // 2),
            pick_copy(c, 5, x_far, z_up),
            pick_copy(c, 6, x_far, z_down),
        ]

    def far_sends(c):
        return [pick_copy(c, 7, z_far, x_far)]

    def near_arrivals(c):
        return [
            pick_copy(c, 0, z_down, z_up),
            pick_copy(c, 1, z_up, z_down),
            pick_copy(c, 2, x_far, x_far),
        ]

    def half_arrivals(c):
        return [
            pick_copy(c, 3, z_far, z_up, 0),
            pick_copy(c, 4, z_far, z_down, HALF // 2),
        ]

    def last_arrivals(c):
        return [
            pick_copy(c, 5, z_down + other, z_up),
            pick_copy(c, 6, z_up + other, z_down),
            pick_copy(c, 7, z_far + other, x_far),
        ]

    def start_all(copies):
        for copy in copies:
            copy.start()

    def arrive_all(copies):
        for copy in copies:
            copy.wait_recv()

    for copy in go_copies:
        copy.wait()
    sel_wide = jnp.transpose(jnp.broadcast_to(sel_ref[...], (HALF, ROWS)))
    for c in range(2):
        sel_half = sel_wide[c * HALF : (c + 1) * HALF]
        total = jnp.zeros((HALF, WIDE), F32)
        for p in range(4):
            pieces = []
            for b in range(4):
                token = lax.broadcasted_iota(jnp.int32, (HALF, HALF), 1) + (p * 512 + b * 128)
                pieces.append(jnp.where(token == sel_half, 1.0, 0.0).astype(BF))
            chosen = jnp.concatenate(pieces, axis=1)
            total += dot(chosen, probs[p // 2, :, (p % 2) * WIDE : (p % 2 + 1) * WIDE], NN)
        picked[c, t] = total.astype(BF)
        if c == 0:
            start_all(own_sends(0))

    for c in range(2):
        for n in range(GROUP):
            block = q_ref[c * HALF : (c + 1) * HALF, n * HD : (n + 1) * HD]
            at = c * LANES + n * HALF
            q_s[at : at + HALF, :] = block
            q_t[:, at : at + HALF] = jnp.transpose(block)

    def rank_of(c):
        return s * ROWS + c * HALF

    def hidden(k, c):
        key_at = lax.broadcasted_iota(jnp.int32, (512, LANES), 0) + k * 512
        row_at = (lax.broadcasted_iota(jnp.int32, (512, LANES), 1) % HALF) + rank_of(c)
        return key_at > row_at

    def keys_of(k):
        return jnp.concatenate([kv[2 * k, 0], kv[2 * k + 1, 0]], axis=0)

    def values_of(k):
        return jnp.concatenate([kv[2 * k, 1], kv[2 * k + 1, 1]], axis=0)

    top[...] = jnp.full_like(top, FLOOR)

    def first_pass(k, masked):
        keys = keys_of(k)
        for c in range(2):
            lanes = pl.ds(c * LANES, LANES)
            scores = dot(keys, q_t[:, lanes], NN)
            if masked:
                scores = jnp.where(hidden(k, c), FLOOR, scores)
            top[:, lanes] = jnp.maximum(
                top[:, lanes], jnp.max(scores.reshape(64, 8, LANES), axis=0)
            )

    def near_step(c):
        arrive_all(near_arrivals(c))
        start_all(near_sends(c))

    def far_step(c):
        arrive_all(half_arrivals(c))
        start_all(far_sends(c))

    def first_step(d):
        k = (chip + CHIPS - d) % CHIPS

        @pl.when(d > 0)
        def _():
            kv_arrived(k * 2 + core)
            side_copy(d).start()

        kv_arrived(k * 2 + 1 - core)

        @pl.when(d == 0)
        def _():
            first_pass(k, True)

        @pl.when((d > 0) & (k < chip))
        def _():
            first_pass(k, False)

    loop(CHIPS, first_step)
    near_step(0)

    peak = jnp.max(top[...], axis=0, keepdims=True) * SCALE
    top[...] = jnp.broadcast_to(peak, top.shape)
    o_t[...] = jnp.zeros_like(o_t)

    def second_pass(k, masked):
        keys = keys_of(k)
        values_t = jnp.concatenate(
            [jnp.transpose(values_of(k)), jnp.ones((16, 512), BF)], axis=0
        )
        for c in range(2):
            lanes = pl.ds(c * LANES, LANES)
            scores = dot(keys, q_t[:, lanes], NN) * SCALE - top[0:1, lanes]
            if masked:
                scores = jnp.where(hidden(k, c), FLOOR, scores)
            weights = jnp.exp2(scores).astype(BF)
            probs[k, :, lanes] = weights
            o_t[:, lanes] += dot(values_t, weights, NN)

    def second_step(d):
        k = chip - d

        @pl.when(d == 0)
        def _():
            second_pass(k, True)

        @pl.when((d > 0) & (k >= 0))
        def _():
            second_pass(k, False)

        @pl.when(d == 3)
        def _():
            far_step(0)
            start_all(own_sends(1))

    loop(CHIPS, second_step)

    def project(c, slots, fresh):
        total = None
        for slot in slots:
            columns = pl.ds(pl.multiple_of(slot * WIDE, WIDE), WIDE)
            term = dot(w_ref[:, columns], picked[c, slot], NT)
            total = term if total is None else total + term
        if fresh:
            g_t[...] = total
        else:
            g_t[...] += total

    def near_slots():
        return [t, z_down, z_up, x_far]

    def far_slots():
        return [z_far, z_down + other, z_up + other, z_far + other]

    router_part[t] = jnp.zeros((8, HALF), F32)

    def cotangents(c):
        router_row = router_ref[0:1, c * HALF : (c + 1) * HALF]
        router_sum = jnp.zeros((1, HALF), F32)
        for n in range(GROUP):
            at = c * LANES + n * HALF
            g = g_t[n * HD : (n + 1) * HD, :]
            inverse = 1.0 / o_t[HD : HD + 1, at : at + HALF]
            share = jnp.sum(g * o_t[0:HD, at : at + HALF], axis=0, keepdims=True) * inverse
            router_sum += share
            level = router_row * inverse
            delta[0:1, n * HALF : (n + 1) * HALF] = share * level
            scaled = g * level
            do_t[:, n * HALF : (n + 1) * HALF] = scaled.astype(BF)
            do_s[n * HALF : (n + 1) * HALF, :] = jnp.transpose(scaled).astype(BF)
        router_part[t, c : c + 1, :] = router_sum

    def part_copy(j, source):
        return pltpu.make_async_remote_copy(
            src_ref=out_part.at[j],
            dst_ref=in_part.at[source],
            send_sem=part_send.at[j],
            recv_sem=part_recv.at[source],
            device_id=(j, t),
            device_id_type=MESH,
        )

    def backward_step(c, k):
        lanes = pl.ds(c * LANES, LANES)
        keys = keys_of(k)
        weights = probs[k, :, lanes]
        grad_probs = dot(values_of(k), do_t[...], NN) - delta[0:1, :]
        grad_scores = (weights.astype(F32) * grad_probs).astype(BF)
        d_values = dot(weights, do_s[...], NN)
        d_keys = dot(grad_scores, q_s[lanes, :], NN)
        d_queries = dot(keys, grad_scores, TN)
        dq_t[...] += d_queries
        if c == 0:
            acc[k, 0] = d_keys
            acc[k, 1] = d_values
        else:
            d_keys = acc[k, 0] + d_keys
            d_values = acc[k, 1] + d_values
            acc[k, 0] = d_keys
            acc[k, 1] = d_values
            for u in range(2):
                j = 2 * k + u
                out_part[j, 0] = d_keys[u * ROWS : (u + 1) * ROWS].astype(BF)
                out_part[j, 1] = d_values[u * ROWS : (u + 1) * ROWS].astype(BF)

                @pl.when(j < s)
                def _():
                    part_copy(j, s).start()

    def store_queries(c):
        for n in range(GROUP):
            block = jnp.transpose(dq_t[:, n * HALF : (n + 1) * HALF]) * FACTOR
            dq_ref[c * HALF : (c + 1) * HALF, n * HD : (n + 1) * HD] = block.astype(BF)

    def router_copy(step, slot):
        return pltpu.make_async_remote_copy(
            src_ref=router_part.at[slot],
            dst_ref=router_part.at[slot],
            send_sem=router_send.at[step],
            recv_sem=router_recv.at[slot],
            device_id=(s, (t + step) % TP),
            device_id_type=MESH,
        )

    w_copy.wait()
    project(0, near_slots(), True)
    arrive_all(last_arrivals(0))
    project(0, far_slots(), False)
    cotangents(0)
    dq_t[...] = jnp.zeros_like(dq_t)

    def early_step(k):
        @pl.when(k <= chip)
        def _():
            backward_step(0, k)

        @pl.when(k == 1)
        def _():
            near_step(1)

        @pl.when(k == 4)
        def _():
            far_step(1)

    loop(CHIPS, early_step)
    store_queries(0)

    project(1, near_slots(), True)
    arrive_all(last_arrivals(1))
    project(1, far_slots(), False)
    cotangents(1)
    for step in range(1, TP):
        router_copy(step, t).start()
    dq_t[...] = jnp.zeros_like(dq_t)
    loop(chip + 1, lambda k: backward_step(1, k))
    store_queries(1)

    router_total = router_part[t]
    for step in range(1, TP):
        slot = (t + step) % TP
        router_copy(step, slot).wait_recv()
        router_total += router_part[slot]
    gr_ref[...] = router_total

    own = pl.ds(pl.multiple_of(core * ROWS, ROWS), ROWS)
    dk_sum = acc[chip, 0, own, :]
    dv_sum = acc[chip, 1, own, :]
    acc[0, 0, 0:ROWS, :] = dk_sum
    acc[0, 1, 0:ROWS, :] = dv_sum

    def collect(n):
        source = SEQ - 1 - n

        @pl.when(source > s)
        def _():
            part_copy(s, source).wait_recv()
            acc[0, 0, 0:ROWS, :] += in_part[source, 0].astype(F32)
            acc[0, 1, 0:ROWS, :] += in_part[source, 1].astype(F32)

    loop(SEQ, collect)
    dk_ref[...] = (acc[0, 0, 0:ROWS, :] * FACTOR).astype(BF)
    dv_ref[...] = acc[0, 1, 0:ROWS, :].astype(BF)

    side_copy(0).wait_send()
    for step in range(1, CHIPS):
        kv_copy(step).wait_send()
        side_copy(step).wait_send()
    for c in range(2):
        for copy in own_sends(c) + near_sends(c) + far_sends(c):
            copy.wait_send()
    for step in range(1, TP):
        router_copy(step, t).wait_send()

    def sent(j):
        @pl.when(j < s)
        def _():
            part_copy(j, s).wait_send()

    loop(SEQ, sent)


def body(grad_out, select, router, query, key_rows, value_rows, out_weight):
    vmem = pl.BlockSpec(memory_space=pltpu.VMEM)
    hbm = pl.BlockSpec(memory_space=pl.ANY)
    dma = pltpu.SemaphoreType.DMA
    dq, dk, dv, gr = pl.pallas_call(
        kernel,
        out_shape=(
            jax.ShapeDtypeStruct((ROWS, WIDE), BF),
            jax.ShapeDtypeStruct((ROWS, HD), BF),
            jax.ShapeDtypeStruct((ROWS, HD), BF),
            jax.ShapeDtypeStruct((8, HALF), F32),
        ),
        in_specs=[hbm, hbm] + [vmem] * 5,
        out_specs=(vmem,) * 4,
        scratch_shapes=[
            pltpu.VMEM((CHIPS, 512, 2 * LANES), BF),
            pltpu.VMEM((WIDE, TP * WIDE), BF),
            pltpu.VMEM((2, TP, HALF, WIDE), BF),
            pltpu.VMEM((SEQ, 2, ROWS, HD), BF),
            pltpu.VMEM((CHIPS, 2, 512, HD), F32),
            pltpu.VMEM((SEQ, 2, ROWS, HD), BF),
            pltpu.VMEM((SEQ, 2, ROWS, HD), BF),
            pltpu.VMEM((HD, 2 * LANES), BF),
            pltpu.VMEM((2 * LANES, HD), BF),
            pltpu.VMEM((8, 2 * LANES), F32),
            pltpu.VMEM((HD + 16, 2 * LANES), F32),
            pltpu.VMEM((WIDE, HALF), F32),
            pltpu.VMEM((HD, LANES), BF),
            pltpu.VMEM((LANES, HD), BF),
            pltpu.VMEM((8, LANES), F32),
            pltpu.VMEM((HD, LANES), F32),
            pltpu.VMEM((TP, 8, HALF), F32),
            dma((5,)),
            dma((CHIPS,)),
            dma((SEQ,)),
            dma((CHIPS,)),
            dma((2, 8)),
            dma((2, 8)),
            dma((SEQ,)),
            dma((SEQ,)),
            dma((TP,)),
            dma((TP,)),
        ],
        compiler_params=pltpu.CompilerParams(
            collective_id=0, has_side_effects=True, vmem_limit_bytes=62 << 20
        ),
    )(
        grad_out,
        out_weight,
        select.reshape(1, ROWS),
        router.reshape(1, ROWS),
        query,
        key_rows,
        value_rows,
    )
    return dq, dk, dv, gr[0:2].reshape(ROWS)


def solution(mesh):
    return jax.shard_map(
        body,
        mesh=mesh,
        in_specs=(
            P("seq", "tp"),
            P("seq"),
            P("seq"),
            P("seq", "tp"),
            P("seq", "tp"),
            P("seq", "tp"),
            P("tp", None),
        ),
        out_specs=(P("seq", "tp"), P("seq", "tp"), P("seq", "tp"), P("seq")),
        check_vma=False,
    )
```

```python
import math

import jax
import jax.numpy as jnp
from jax import lax
from jax.experimental import pallas as pl
from jax.experimental.pallas import tpu as pltpu
from jax.sharding import PartitionSpec as P

F32 = jnp.float32
BF = jnp.bfloat16
MESH = pl.DeviceIdType.MESH
NN = ((1,), (0,))
NT = ((1,), (1,))
TN = ((0,), (0,))

HD = 128
GROUP = 8
SEQ = 16
TP = 8
CHIPS = 8
ROWS = 256
HALF = 128
LANES = 2048
WIDE = 1024
FACTOR = 1.0 / math.sqrt(HD)
SCALE = FACTOR * math.log2(math.e)
FLOOR = -1e30


def dot(a, b, dims):
    return lax.dot_general(a, b, (dims, ((), ())), preferred_element_type=F32)


def loop(count, step):
    def run(i, carry):
        step(i)
        return carry

    lax.fori_loop(0, count, run, 0)


def loop_from(first, last, step):
    def run(i, carry):
        step(i)
        return carry

    lax.fori_loop(first, last, run, 0)


def kernel(
    go_hbm,
    w_hbm,
    sel_ref,
    router_ref,
    q_ref,
    k_ref,
    v_ref,
    dq_ref,
    dk_ref,
    dv_ref,
    gr_ref,
    probs,
    w_ref,
    picked,
    keys,
    values,
    acc,
    out_side,
    in_side,
    out_part,
    in_part,
    q_t,
    q_s,
    top,
    o_t,
    g_t,
    do_t,
    do_s,
    delta,
    dq_t,
    router_part,
    local_sem,
    kv_send,
    kv_recv,
    side_send,
    pick_send,
    pick_recv,
    fold_send,
    fold_recv,
    part_send,
    part_recv,
    router_send,
    router_recv,
):
    s = lax.axis_index("seq")
    t = lax.axis_index("tp")
    chip = s // 2
    core = s % 2
    y = chip // 2
    xl = chip % 2
    z = t // 2
    h = t % 2
    sibling = s + 1 - 2 * core
    z_up = ((z + 1) % 4) * 2 + h
    z_down = ((z + 3) % 4) * 2 + h
    z_far = ((z + 2) % 4) * 2 + h
    x_far = z * 2 + 1 - h
    other = 1 - 2 * h

    def remote(src, dst, send, recv, to):
        return pltpu.make_async_remote_copy(
            src_ref=src,
            dst_ref=dst,
            send_sem=send,
            recv_sem=recv,
            device_id=to,
            device_id_type=MESH,
        )

    go_copies = []
    for p in range(4):
        go_copies.append(
            pltpu.make_async_copy(
                go_hbm.at[pl.ds(p * 512, 512), :],
                probs.at[p // 2, :, pl.ds((p % 2) * WIDE, WIDE)],
                local_sem.at[p],
            )
        )
    for copy in go_copies:
        copy.start()
    w_copy = pltpu.make_async_copy(w_hbm, w_ref, local_sem.at[4])
    w_copy.start()

    barrier = pltpu.get_barrier_semaphore()
    pl.semaphore_signal(barrier, inc=1, device_id=(sibling, t), device_id_type=MESH)
    for step in range(1, CHIPS):
        pl.semaphore_signal(
            barrier,
            inc=1,
            device_id=(((chip + step) % CHIPS) * 2 + core, t),
            device_id_type=MESH,
        )
    for step in range(1, TP):
        pl.semaphore_signal(
            barrier, inc=1, device_id=(s, (t + step) % TP), device_id_type=MESH
        )
    mine = pl.ds(pl.multiple_of(core * ROWS, ROWS), ROWS)
    theirs = pl.ds(pl.multiple_of((1 - core) * ROWS, ROWS), ROWS)
    keys[chip, mine, :] = k_ref[...]
    values[chip, mine, :] = v_ref[...]

    def choose(c):
        sel_half = jnp.transpose(
            jnp.broadcast_to(sel_ref[0:1, c * HALF : (c + 1) * HALF], (HALF, HALF))
        )
        total = jnp.zeros((HALF, WIDE), F32)
        for p in range(4):
            pieces = []
            for b in range(4):
                token = lax.broadcasted_iota(jnp.int32, (HALF, HALF), 1) + (p * 512 + b * 128)
                pieces.append(jnp.where(token == sel_half, 1.0, 0.0).astype(BF))
            chosen = jnp.concatenate(pieces, axis=1)
            total += dot(chosen, probs[p // 2, :, (p % 2) * WIDE : (p % 2 + 1) * WIDE], NN)
        picked[t, c * HALF : (c + 1) * HALF, :] = total.astype(BF)

    for copy in go_copies:
        copy.wait()
    choose(0)
    pl.semaphore_wait(barrier, CHIPS + TP - 1)

    def block_of(i, block):
        rows = pl.ds(pl.multiple_of((block % 2) * ROWS, ROWS), ROWS)
        return (keys, values)[i].at[block // 2, rows, :]

    def kv_copy(i, n, block, to):
        part = block_of(i, block)
        return remote(part, part, kv_send.at[i, n], kv_recv.at[i, block], (to, t))

    def later_chips(i, act):
        for step in range(1, CHIPS):

            @pl.when(chip + step < CHIPS)
            def _(step=step):
                act(kv_copy(i, step, s, (chip + step) * 2 + core))

    def side_copy(i, d):
        block = (chip - d) * 2 + core
        part = block_of(i, block)
        return remote(part, part, side_send.at[i, d], kv_recv.at[i, block], (sibling, t))

    def kv_ahead(i, d):
        @pl.when(d <= chip)
        def _():
            kv_copy(i, 0, (chip - d) * 2 + core, sibling).wait_recv()
            side_copy(i, d).start()

    def kv_arrived(i, d):
        kv_copy(i, 0, (chip - d) * 2 + 1 - core, sibling).wait_recv()

    def start_all(copies):
        for copy in copies:
            copy.start()

    def arrive_all(copies):
        for copy in copies:
            copy.wait_recv()

    side_copy(0, 0).start()
    later_chips(0, lambda copy: copy.start())
    side_copy(1, 0).start()

    def pick_copy(c, n, slot, to, at=0, rows=HALF):
        src = picked.at[slot, pl.ds(c * HALF + at, rows), :]
        return remote(src, src, pick_send.at[c, n], pick_recv.at[c, n], (s, to))

    quarter = HALF // 2

    def own_sends(c):
        return [
            pick_copy(c, 2, t, x_far),
            pick_copy(c, 0, t, z_up),
            pick_copy(c, 1, t, z_down),
        ]

    def half_sends(c):
        return [
            pick_copy(c, 3, z_down, z_up, 0, quarter),
            pick_copy(c, 4, z_up, z_down, quarter, quarter),
        ]

    def cross_sends(c):
        return [pick_copy(c, 5, x_far, z_up), pick_copy(c, 6, x_far, z_down)]

    def far_sends(c):
        return [pick_copy(c, 7, z_far, x_far)]

    def near_arrivals(c):
        return [pick_copy(c, 0, z_down, z_up), pick_copy(c, 1, z_up, z_down)]

    def x_arrivals(c):
        return [pick_copy(c, 2, x_far, x_far)]

    def half_arrivals(c):
        return [
            pick_copy(c, 3, z_far, z_up, 0, quarter),
            pick_copy(c, 4, z_far, z_down, quarter, quarter),
        ]

    def cross_arrivals(c):
        return [
            pick_copy(c, 5, z_down + other, z_up),
            pick_copy(c, 6, z_up + other, z_down),
        ]

    def far_arrivals(c):
        return [pick_copy(c, 7, z_far + other, x_far)]

    start_all(own_sends(0))
    choose(1)
    start_all(own_sends(1))
    later_chips(1, lambda copy: copy.start())

    for n in range(GROUP):
        block = q_ref[:, n * HD : (n + 1) * HD]
        q_s[n * ROWS : (n + 1) * ROWS, :] = block
        q_t[:, n * ROWS : (n + 1) * ROWS] = jnp.transpose(block)

    def hidden(k):
        key_at = lax.broadcasted_iota(jnp.int32, (512, LANES), 0) + k * 512
        row_at = (lax.broadcasted_iota(jnp.int32, (512, LANES), 1) % ROWS) + s * ROWS
        return key_at > row_at

    top[...] = jnp.full_like(top, FLOOR)

    def first_pass(k, masked):
        scores = dot(keys[k], q_t[...], NN)
        if masked:
            scores = jnp.where(hidden(k), FLOOR, scores)
        top[...] = jnp.maximum(top[...], jnp.max(scores.reshape(64, 8, LANES), axis=0))

    def first_step(d):
        kv_ahead(0, d + 1)

        @pl.when(d <= chip)
        def _():
            kv_arrived(0, d)
            first_pass(chip - d, False)

        @pl.when(d == 5)
        def _():
            arrive_all(near_arrivals(0))
            start_all(half_sends(0))

    kv_arrived(0, 0)
    kv_ahead(0, 1)
    first_pass(chip, True)
    loop_from(1, CHIPS, first_step)
    kv_ahead(1, 1)

    peak = jnp.max(top[...], axis=0, keepdims=True) * SCALE
    top[...] = jnp.broadcast_to(peak, top.shape)
    o_t[...] = jnp.zeros_like(o_t)

    def second_pass(k, masked):
        values_t = jnp.concatenate(
            [jnp.transpose(values[k]), jnp.ones((16, 512), BF)], axis=0
        )
        scores = dot(keys[k], q_t[...], NN) * SCALE - top[0:1, :]
        if masked:
            scores = jnp.where(hidden(k), FLOOR, scores)
        weights = jnp.exp2(scores).astype(BF)
        probs[k] = weights
        o_t[...] += dot(values_t, weights, NN)

    def second_step(d):
        kv_ahead(1, d + 1)

        @pl.when(d <= chip)
        def _():
            kv_arrived(1, d)
            second_pass(chip - d, False)

        @pl.when(d == 2)
        def _():
            arrive_all(near_arrivals(1))
            start_all(half_sends(1))
            arrive_all(x_arrivals(0))
            start_all(cross_sends(0))
            arrive_all(x_arrivals(1))
            start_all(cross_sends(1))

        @pl.when(d == 5)
        def _():
            arrive_all(half_arrivals(0))
            start_all(far_sends(0))

    kv_arrived(1, 0)
    second_pass(chip, True)
    loop_from(1, CHIPS, second_step)
    arrive_all(half_arrivals(1))
    start_all(far_sends(1))

    def project(slot, fresh=False):
        columns = pl.ds(pl.multiple_of(slot * WIDE, WIDE), WIDE)
        term = dot(w_ref[:, columns], picked[slot], NT)
        if fresh:
            g_t[...] = term
        else:
            g_t[...] += term

    w_copy.wait()
    project(t, True)
    project(z_down)
    project(z_up)
    project(x_far)
    project(z_far)
    arrive_all(cross_arrivals(0) + cross_arrivals(1))
    project(z_down + other)
    project(z_up + other)
    arrive_all(far_arrivals(0) + far_arrivals(1))
    project(z_far + other)

    router_row = router_ref[...]
    router_sum = jnp.zeros((1, ROWS), F32)
    for n in range(GROUP):
        lanes = slice(n * ROWS, (n + 1) * ROWS)
        g = g_t[n * HD : (n + 1) * HD, :]
        inverse = 1.0 / o_t[HD : HD + 1, lanes]
        share = jnp.sum(g * o_t[0:HD, lanes], axis=0, keepdims=True) * inverse
        router_sum += share
        level = router_row * inverse
        delta[0:1, lanes] = share * level
        scaled = g * level
        do_t[:, lanes] = scaled.astype(BF)
        do_s[lanes, :] = jnp.transpose(scaled).astype(BF)
    router_part[t] = jnp.broadcast_to(router_sum, (8, ROWS))

    def router_copy(step, slot):
        part = router_part.at[slot]
        return remote(
            part, part, router_send.at[step], router_recv.at[slot], (s, (t + step) % TP)
        )

    for step in range(1, TP):
        router_copy(step, t).start()

    def fold_copy(k):
        return remote(
            out_side.at[k], in_side.at[k], fold_send.at[k], fold_recv.at[k], (sibling, t)
        )

    def part_copy(k, source):
        return remote(
            out_part.at[k],
            in_part.at[source],
            part_send.at[k],
            part_recv.at[source],
            (k * 2 + core, t),
        )

    def backward_step(k):
        weights = probs[k]
        grad_probs = dot(values[k], do_t[...], NN) - delta[0:1, :]
        grad_scores = (weights.astype(F32) * grad_probs).astype(BF)
        acc[k, 1] = dot(weights, do_s[...], NN)
        acc[k, 0] = dot(grad_scores, q_s[...], NN)
        probs[k] = grad_scores
        for n in range(2):
            out_side[k, n] = acc[k, n, theirs, :].astype(BF)
        fold_copy(k).start()

    def fold(k):
        fold_copy(k).wait_recv()
        for n in range(2):
            acc[k, n, mine, :] += in_side[k, n].astype(F32)

    def pass_on(k):
        fold(k)
        for n in range(2):
            out_part[k, n] = acc[k, n, mine, :].astype(BF)
        part_copy(k, chip).start()

    def backward(k):
        backward_step(k)

        @pl.when(k > 1)
        def _():
            pass_on(k - 2)

    loop(chip + 1, backward)

    @pl.when(chip > 0)
    def _():
        pass_on(chip - 1)

    dq_t[...] = jnp.zeros_like(dq_t)

    def query_step(k):
        dq_t[...] += dot(keys[k], probs[k], TN)

    loop(chip + 1, query_step)
    for n in range(GROUP):
        block = jnp.transpose(dq_t[:, n * ROWS : (n + 1) * ROWS]) * FACTOR
        dq_ref[:, n * HD : (n + 1) * HD] = block.astype(BF)

    router_total = router_part[t]
    for step in range(1, TP):
        slot = (t + step) % TP
        router_copy(step, slot).wait_recv()
        router_total += router_part[slot]
    gr_ref[...] = router_total

    fold(chip)

    def collect(n):
        source = CHIPS - 1 - n

        @pl.when(source > chip)
        def _():
            part_copy(chip, source).wait_recv()
            for i in range(2):
                acc[chip, i, mine, :] += in_part[source, i].astype(F32)

    loop(CHIPS, collect)
    dk_ref[...] = (acc[chip, 0, mine, :] * FACTOR).astype(BF)
    dv_ref[...] = acc[chip, 1, mine, :].astype(BF)

    for i in range(2):
        later_chips(i, lambda copy: copy.wait_send())
    for c in range(2):
        for copy in own_sends(c) + half_sends(c) + cross_sends(c) + far_sends(c):
            copy.wait_send()
    for step in range(1, TP):
        router_copy(step, t).wait_send()

    def sent(k):
        @pl.when(k <= chip)
        def _():
            side_copy(0, k).wait_send()
            side_copy(1, k).wait_send()
            fold_copy(k).wait_send()

        @pl.when(k < chip)
        def _():
            part_copy(k, chip).wait_send()

    loop(CHIPS, sent)


def place(dq_in, dk_in, dv_in, gr_in, dq_ref, dk_ref, dv_ref, gr_ref, sem):
    copies = [
        pltpu.make_async_copy(dq_in, dq_ref, sem.at[0]),
        pltpu.make_async_copy(dk_in, dk_ref, sem.at[1]),
        pltpu.make_async_copy(dv_in, dv_ref, sem.at[2]),
    ]
    for copy in copies:
        copy.start()
    gr_ref[...] = gr_in[0:1, :]
    for copy in copies:
        copy.wait()


def body(grad_out, select, router, query, key_rows, value_rows, out_weight):
    vmem = pl.BlockSpec(memory_space=pltpu.VMEM)
    hbm = pl.BlockSpec(memory_space=pl.ANY)
    dma = pltpu.SemaphoreType.DMA
    shapes = (
        jax.ShapeDtypeStruct((ROWS, WIDE), BF),
        jax.ShapeDtypeStruct((ROWS, HD), BF),
        jax.ShapeDtypeStruct((ROWS, HD), BF),
    )
    parts = pl.pallas_call(
        kernel,
        out_shape=shapes + (jax.ShapeDtypeStruct((8, ROWS), F32),),
        in_specs=[hbm, hbm] + [vmem] * 5,
        out_specs=(vmem,) * 4,
        scratch_shapes=[
            pltpu.VMEM((CHIPS, 512, LANES), BF),
            pltpu.VMEM((WIDE, TP * WIDE), BF),
            pltpu.VMEM((TP, ROWS, WIDE), BF),
            pltpu.VMEM((CHIPS, 512, HD), BF),
            pltpu.VMEM((CHIPS, 512, HD), BF),
            pltpu.VMEM((CHIPS, 2, 512, HD), F32),
            pltpu.VMEM((CHIPS, 2, ROWS, HD), BF),
            pltpu.VMEM((CHIPS, 2, ROWS, HD), BF),
            pltpu.VMEM((CHIPS, 2, ROWS, HD), BF),
            pltpu.VMEM((CHIPS, 2, ROWS, HD), BF),
            pltpu.VMEM((HD, LANES), BF),
            pltpu.VMEM((LANES, HD), BF),
            pltpu.VMEM((8, LANES), F32),
            pltpu.VMEM((HD + 16, LANES), F32),
            pltpu.VMEM((WIDE, ROWS), F32),
            pltpu.VMEM((HD, LANES), BF),
            pltpu.VMEM((LANES, HD), BF),
            pltpu.VMEM((8, LANES), F32),
            pltpu.VMEM((HD, LANES), F32),
            pltpu.VMEM((TP, 8, ROWS), F32),
            dma((5,)),
            dma((2, CHIPS)),
            dma((2, SEQ)),
            dma((2, CHIPS)),
            dma((2, 8)),
            dma((2, 8)),
            dma((CHIPS,)),
            dma((CHIPS,)),
            dma((CHIPS,)),
            dma((CHIPS,)),
            dma((TP,)),
            dma((TP,)),
        ],
        compiler_params=pltpu.CompilerParams(
            collective_id=0, has_side_effects=True, vmem_limit_bytes=62 << 20
        ),
    )(
        grad_out,
        out_weight,
        select.reshape(1, ROWS),
        router.reshape(1, ROWS),
        query,
        key_rows,
        value_rows,
    )
    dq, dk, dv, gr = pl.pallas_call(
        place,
        out_shape=shapes + (jax.ShapeDtypeStruct((1, ROWS), F32),),
        in_specs=[vmem] * 4,
        out_specs=(hbm,) * 3 + (vmem,),
        scratch_shapes=[dma((3,))],
    )(*parts)
    return dq, dk, dv, gr.reshape(ROWS)


def solution(mesh):
    return jax.shard_map(
        body,
        mesh=mesh,
        in_specs=(
            P("seq", "tp"),
            P("seq"),
            P("seq"),
            P("seq", "tp"),
            P("seq", "tp"),
            P("seq", "tp"),
            P("tp", None),
        ),
        out_specs=(P("seq", "tp"), P("seq", "tp"), P("seq", "tp"), P("seq")),
        check_vma=False,
    )
```

```python
import math

import jax
import jax.numpy as jnp
from jax import lax
from jax.experimental import pallas as pl
from jax.experimental.pallas import tpu as pltpu
from jax.sharding import PartitionSpec as P

F32 = jnp.float32
BF = jnp.bfloat16
MESH = pl.DeviceIdType.MESH
NN = ((1,), (0,))
NT = ((1,), (1,))
TN = ((0,), (0,))

HD = 128
GROUP = 8
SEQ = 16
TP = 8
CHIPS = 8
ROWS = 256
HALF = 128
LANES = 2048
WIDE = 1024
FACTOR = 1.0 / math.sqrt(HD)
SCALE = FACTOR * math.log2(math.e)
FLOOR = -1e30


def dot(a, b, dims):
    return lax.dot_general(a, b, (dims, ((), ())), preferred_element_type=F32)


def loop(count, step):
    def run(i, carry):
        step(i)
        return carry

    lax.fori_loop(0, count, run, 0)


def loop_from(first, last, step):
    def run(i, carry):
        step(i)
        return carry

    lax.fori_loop(first, last, run, 0)


def kernel(
    go_hbm,
    w_hbm,
    sel_ref,
    router_ref,
    q_hbm,
    k_hbm,
    v_hbm,
    dq_ref,
    dk_ref,
    dv_ref,
    gr_ref,
    probs,
    w_ref,
    picked,
    keys,
    values,
    acc,
    out_side,
    in_side,
    out_part,
    in_part,
    q_ref,
    q_t,
    q_s,
    top,
    o_t,
    g_t,
    do_t,
    do_s,
    delta,
    dq_t,
    router_part,
    local_sem,
    kv_send,
    kv_recv,
    side_send,
    pick_send,
    pick_recv,
    fold_send,
    fold_recv,
    part_send,
    part_recv,
    router_send,
    router_recv,
):
    s = lax.axis_index("seq")
    t = lax.axis_index("tp")
    chip = s // 2
    core = s % 2
    y = chip // 2
    xl = chip % 2
    z = t // 2
    h = t % 2
    sibling = s + 1 - 2 * core
    z_up = ((z + 1) % 4) * 2 + h
    z_down = ((z + 3) % 4) * 2 + h
    z_far = ((z + 2) % 4) * 2 + h
    x_far = z * 2 + 1 - h
    other = 1 - 2 * h

    def remote(src, dst, send, recv, to):
        return pltpu.make_async_remote_copy(
            src_ref=src,
            dst_ref=dst,
            send_sem=send,
            recv_sem=recv,
            device_id=to,
            device_id_type=MESH,
        )

    mine = pl.ds(pl.multiple_of(core * ROWS, ROWS), ROWS)
    theirs = pl.ds(pl.multiple_of((1 - core) * ROWS, ROWS), ROWS)
    kv_inputs = [
        pltpu.make_async_copy(k_hbm, keys.at[chip, mine, :], local_sem.at[5]),
        pltpu.make_async_copy(v_hbm, values.at[chip, mine, :], local_sem.at[6]),
    ]
    for copy in kv_inputs:
        copy.start()
    go_copies = []
    for p in range(4):
        go_copies.append(
            pltpu.make_async_copy(
                go_hbm.at[pl.ds(p * 512, 512), :],
                probs.at[p // 2, :, pl.ds((p % 2) * WIDE, WIDE)],
                local_sem.at[p],
            )
        )
    for copy in go_copies:
        copy.start()
    w_copy = pltpu.make_async_copy(w_hbm, w_ref, local_sem.at[4])
    q_copy = pltpu.make_async_copy(q_hbm, q_ref, local_sem.at[7])
    q_copy.start()

    barrier = pltpu.get_barrier_semaphore()
    pl.semaphore_signal(barrier, inc=1, device_id=(sibling, t), device_id_type=MESH)
    for step in range(1, CHIPS):
        pl.semaphore_signal(
            barrier,
            inc=1,
            device_id=(((chip + step) % CHIPS) * 2 + core, t),
            device_id_type=MESH,
        )
    for step in range(1, TP):
        pl.semaphore_signal(
            barrier, inc=1, device_id=(s, (t + step) % TP), device_id_type=MESH
        )

    def choose(c):
        sel_half = jnp.transpose(
            jnp.broadcast_to(sel_ref[0:1, c * HALF : (c + 1) * HALF], (HALF, HALF))
        )
        total = jnp.zeros((HALF, WIDE), F32)
        for p in range(4):
            pieces = []
            for b in range(4):
                token = lax.broadcasted_iota(jnp.int32, (HALF, HALF), 1) + (p * 512 + b * 128)
                pieces.append(jnp.where(token == sel_half, 1.0, 0.0).astype(BF))
            chosen = jnp.concatenate(pieces, axis=1)
            total += dot(chosen, probs[p // 2, :, (p % 2) * WIDE : (p % 2 + 1) * WIDE], NN)
        picked[t, c * HALF : (c + 1) * HALF, :] = total.astype(BF)

    for copy in go_copies:
        copy.wait()
    choose(0)
    for copy in kv_inputs:
        copy.wait()
    pl.semaphore_wait(barrier, CHIPS + TP - 1)

    def block_of(i, block):
        rows = pl.ds(pl.multiple_of((block % 2) * ROWS, ROWS), ROWS)
        return (keys, values)[i].at[block // 2, rows, :]

    def kv_copy(i, n, block, to):
        part = block_of(i, block)
        return remote(part, part, kv_send.at[i, n], kv_recv.at[i, block], (to, t))

    def later_chips(i, act):
        for step in range(1, CHIPS):

            @pl.when(chip + step < CHIPS)
            def _(step=step):
                act(kv_copy(i, step, s, (chip + step) * 2 + core))

    def side_copy(i, d):
        block = (chip - d) * 2 + core
        part = block_of(i, block)
        return remote(part, part, side_send.at[i, d], kv_recv.at[i, block], (sibling, t))

    def kv_ahead(i, d):
        @pl.when(d <= chip)
        def _():
            kv_copy(i, 0, (chip - d) * 2 + core, sibling).wait_recv()
            side_copy(i, d).start()

    def kv_arrived(i, d):
        kv_copy(i, 0, (chip - d) * 2 + 1 - core, sibling).wait_recv()

    def start_all(copies):
        for copy in copies:
            copy.start()

    def arrive_all(copies):
        for copy in copies:
            copy.wait_recv()

    side_copy(0, 0).start()
    later_chips(0, lambda copy: copy.start())
    side_copy(1, 0).start()

    def pick_copy(c, n, slot, to, at=0, rows=HALF):
        src = picked.at[slot, pl.ds(c * HALF + at, rows), :]
        return remote(src, src, pick_send.at[c, n], pick_recv.at[c, n], (s, to))

    quarter = HALF // 2

    def own_sends(c):
        return [
            pick_copy(c, 2, t, x_far),
            pick_copy(c, 0, t, z_up),
            pick_copy(c, 1, t, z_down),
        ]

    def half_sends(c):
        return [
            pick_copy(c, 3, z_down, z_up, 0, quarter),
            pick_copy(c, 4, z_up, z_down, quarter, quarter),
        ]

    def cross_sends(c):
        return [pick_copy(c, 5, x_far, z_up), pick_copy(c, 6, x_far, z_down)]

    def far_sends(c):
        return [pick_copy(c, 7, z_far, x_far)]

    def near_arrivals(c):
        return [pick_copy(c, 0, z_down, z_up), pick_copy(c, 1, z_up, z_down)]

    def x_arrivals(c):
        return [pick_copy(c, 2, x_far, x_far)]

    def half_arrivals(c):
        return [
            pick_copy(c, 3, z_far, z_up, 0, quarter),
            pick_copy(c, 4, z_far, z_down, quarter, quarter),
        ]

    def cross_arrivals(c):
        return [
            pick_copy(c, 5, z_down + other, z_up),
            pick_copy(c, 6, z_up + other, z_down),
        ]

    def far_arrivals(c):
        return [pick_copy(c, 7, z_far + other, x_far)]

    start_all(own_sends(0))
    choose(1)
    w_copy.start()
    later_chips(1, lambda copy: copy.start())

    q_copy.wait()
    for n in range(GROUP):
        block = q_ref[:, n * HD : (n + 1) * HD]
        q_s[n * ROWS : (n + 1) * ROWS, :] = block
        q_t[:, n * ROWS : (n + 1) * ROWS] = jnp.transpose(block)

    def hidden(k):
        key_at = lax.broadcasted_iota(jnp.int32, (512, LANES), 0) + k * 512
        row_at = (lax.broadcasted_iota(jnp.int32, (512, LANES), 1) % ROWS) + s * ROWS
        return key_at > row_at

    top[...] = jnp.full_like(top, FLOOR)

    def first_pass(k, masked):
        scores = dot(keys[k], q_t[...], NN)
        if masked:
            scores = jnp.where(hidden(k), FLOOR, scores)
        top[...] = jnp.maximum(top[...], jnp.max(scores.reshape(64, 8, LANES), axis=0))

    def first_step(d):
        kv_ahead(0, d + 1)

        @pl.when(d <= chip)
        def _():
            kv_arrived(0, d)
            first_pass(chip - d, False)

        @pl.when(d == 2)
        def _():
            arrive_all(near_arrivals(0))
            start_all(half_sends(0))

    start_all(own_sends(1))
    kv_arrived(0, 0)
    first_pass(chip, True)
    kv_ahead(0, 1)
    loop_from(1, CHIPS, first_step)
    kv_ahead(1, 1)

    peak = jnp.max(top[...], axis=0, keepdims=True) * SCALE
    top[...] = jnp.broadcast_to(peak, top.shape)
    o_t[...] = jnp.zeros_like(o_t)

    def second_pass(k, masked):
        values_t = jnp.concatenate(
            [jnp.transpose(values[k]), jnp.ones((16, 512), BF)], axis=0
        )
        scores = dot(keys[k], q_t[...], NN) * SCALE - top[0:1, :]
        if masked:
            scores = jnp.where(hidden(k), FLOOR, scores)
        weights = jnp.exp2(scores).astype(BF)
        probs[k] = weights
        o_t[...] += dot(values_t, weights, NN)

    def second_step(d):
        kv_ahead(1, d + 1)

        @pl.when(d <= chip)
        def _():
            kv_arrived(1, d)
            second_pass(chip - d, False)

        @pl.when(d == 1)
        def _():
            arrive_all(half_arrivals(0))
            start_all(far_sends(0))

        @pl.when(d == 2)
        def _():
            arrive_all(half_arrivals(1))
            start_all(far_sends(1))

    arrive_all(near_arrivals(1))
    start_all(half_sends(1))
    for c in range(2):
        arrive_all(x_arrivals(c))
        start_all(cross_sends(c))
    kv_arrived(1, 0)
    second_pass(chip, True)
    loop_from(1, CHIPS, second_step)

    def project(slot, fresh=False):
        columns = pl.ds(pl.multiple_of(slot * WIDE, WIDE), WIDE)
        term = dot(w_ref[:, columns], picked[slot], NT)
        if fresh:
            g_t[...] = term
        else:
            g_t[...] += term

    w_copy.wait()
    project(t, True)
    project(z_down)
    project(z_up)
    project(x_far)
    project(z_far)
    arrive_all(cross_arrivals(0) + cross_arrivals(1))
    project(z_down + other)
    project(z_up + other)
    arrive_all(far_arrivals(0) + far_arrivals(1))
    project(z_far + other)

    router_row = router_ref[...]
    router_sum = jnp.zeros((1, ROWS), F32)
    for n in range(GROUP):
        lanes = slice(n * ROWS, (n + 1) * ROWS)
        g = g_t[n * HD : (n + 1) * HD, :]
        inverse = 1.0 / o_t[HD : HD + 1, lanes]
        share = jnp.sum(g * o_t[0:HD, lanes], axis=0, keepdims=True) * inverse
        router_sum += share
        level = router_row * inverse
        delta[0:1, lanes] = share * level
        scaled = g * level
        do_t[:, lanes] = scaled.astype(BF)
        do_s[lanes, :] = jnp.transpose(scaled).astype(BF)
    router_part[t] = jnp.broadcast_to(router_sum, (8, ROWS))

    def router_copy(step, slot):
        part = router_part.at[slot]
        return remote(
            part, part, router_send.at[step], router_recv.at[slot], (s, (t + step) % TP)
        )

    for step in range(1, TP):
        router_copy(step, t).start()

    def fold_copy(k):
        return remote(
            out_side.at[k], in_side.at[k], fold_send.at[k], fold_recv.at[k], (sibling, t)
        )

    def part_copy(k, source):
        return remote(
            out_part.at[k],
            in_part.at[source],
            part_send.at[k],
            part_recv.at[source],
            (k * 2 + core, t),
        )

    def backward_step(k):
        weights = probs[k]
        grad_probs = dot(values[k], do_t[...], NN) - delta[0:1, :]
        grad_scores = (weights.astype(F32) * grad_probs).astype(BF)
        acc[k, 1] = dot(weights, do_s[...], NN)
        acc[k, 0] = dot(grad_scores, q_s[...], NN)
        probs[k] = grad_scores
        for n in range(2):
            out_side[k, n] = acc[k, n, theirs, :].astype(BF)
        fold_copy(k).start()

    def fold(k):
        fold_copy(k).wait_recv()
        for n in range(2):
            acc[k, n, mine, :] += in_side[k, n].astype(F32)

    def pass_on(k):
        fold(k)
        for n in range(2):
            out_part[k, n] = acc[k, n, mine, :].astype(BF)
        part_copy(k, chip).start()

    def backward(k):
        backward_step(k)

        @pl.when(k > 0)
        def _():
            pass_on(k - 1)

    loop(chip + 1, backward)

    dq_t[...] = jnp.zeros_like(dq_t)

    def query_step(k):
        dq_t[...] += dot(keys[k], probs[k], TN)

    loop(chip + 1, query_step)
    for n in range(GROUP):
        block = jnp.transpose(dq_t[:, n * ROWS : (n + 1) * ROWS]) * FACTOR
        dq_ref[:, n * HD : (n + 1) * HD] = block.astype(BF)

    router_total = router_part[t]
    for step in range(1, TP):
        slot = (t + step) % TP
        router_copy(step, slot).wait_recv()
        router_total += router_part[slot]
    gr_ref[...] = router_total

    fold(chip)

    def collect(n):
        source = CHIPS - 1 - n

        @pl.when(source > chip)
        def _():
            part_copy(chip, source).wait_recv()
            for i in range(2):
                acc[chip, i, mine, :] += in_part[source, i].astype(F32)

    loop(CHIPS, collect)
    dk_ref[...] = (acc[chip, 0, mine, :] * FACTOR).astype(BF)
    dv_ref[...] = acc[chip, 1, mine, :].astype(BF)

    for i in range(2):
        later_chips(i, lambda copy: copy.wait_send())
    for c in range(2):
        for copy in own_sends(c) + half_sends(c) + cross_sends(c) + far_sends(c):
            copy.wait_send()
    for step in range(1, TP):
        router_copy(step, t).wait_send()

    def sent(k):
        @pl.when(k <= chip)
        def _():
            side_copy(0, k).wait_send()
            side_copy(1, k).wait_send()
            fold_copy(k).wait_send()

        @pl.when(k < chip)
        def _():
            part_copy(k, chip).wait_send()

    loop(CHIPS, sent)


def place(dq_in, dk_in, dv_in, gr_in, dq_ref, dk_ref, dv_ref, gr_ref, sem):
    copies = [
        pltpu.make_async_copy(dq_in, dq_ref, sem.at[0]),
        pltpu.make_async_copy(dk_in, dk_ref, sem.at[1]),
        pltpu.make_async_copy(dv_in, dv_ref, sem.at[2]),
    ]
    for copy in copies:
        copy.start()
    gr_ref[...] = gr_in[0:1, :]
    for copy in copies:
        copy.wait()


def body(grad_out, select, router, query, key_rows, value_rows, out_weight):
    vmem = pl.BlockSpec(memory_space=pltpu.VMEM)
    hbm = pl.BlockSpec(memory_space=pl.ANY)
    dma = pltpu.SemaphoreType.DMA
    shapes = (
        jax.ShapeDtypeStruct((ROWS, WIDE), BF),
        jax.ShapeDtypeStruct((ROWS, HD), BF),
        jax.ShapeDtypeStruct((ROWS, HD), BF),
    )
    parts = pl.pallas_call(
        kernel,
        out_shape=shapes + (jax.ShapeDtypeStruct((8, ROWS), F32),),
        in_specs=[hbm, hbm, vmem, vmem, hbm, hbm, hbm],
        out_specs=(vmem,) * 4,
        scratch_shapes=[
            pltpu.VMEM((CHIPS, 512, LANES), BF),
            pltpu.VMEM((WIDE, TP * WIDE), BF),
            pltpu.VMEM((TP, ROWS, WIDE), BF),
            pltpu.VMEM((CHIPS, 512, HD), BF),
            pltpu.VMEM((CHIPS, 512, HD), BF),
            pltpu.VMEM((CHIPS, 2, 512, HD), F32),
            pltpu.VMEM((CHIPS, 2, ROWS, HD), BF),
            pltpu.VMEM((CHIPS, 2, ROWS, HD), BF),
            pltpu.VMEM((CHIPS, 2, ROWS, HD), BF),
            pltpu.VMEM((CHIPS, 2, ROWS, HD), BF),
            pltpu.VMEM((ROWS, WIDE), BF),
            pltpu.VMEM((HD, LANES), BF),
            pltpu.VMEM((LANES, HD), BF),
            pltpu.VMEM((8, LANES), F32),
            pltpu.VMEM((HD + 16, LANES), F32),
            pltpu.VMEM((WIDE, ROWS), F32),
            pltpu.VMEM((HD, LANES), BF),
            pltpu.VMEM((LANES, HD), BF),
            pltpu.VMEM((8, LANES), F32),
            pltpu.VMEM((HD, LANES), F32),
            pltpu.VMEM((TP, 8, ROWS), F32),
            dma((8,)),
            dma((2, CHIPS)),
            dma((2, SEQ)),
            dma((2, CHIPS)),
            dma((2, 8)),
            dma((2, 8)),
            dma((CHIPS,)),
            dma((CHIPS,)),
            dma((CHIPS,)),
            dma((CHIPS,)),
            dma((TP,)),
            dma((TP,)),
        ],
        compiler_params=pltpu.CompilerParams(
            collective_id=0, has_side_effects=True, vmem_limit_bytes=62 << 20
        ),
    )(
        grad_out,
        out_weight,
        select.reshape(1, ROWS),
        router.reshape(1, ROWS),
        query,
        key_rows,
        value_rows,
    )
    dq, dk, dv, gr = pl.pallas_call(
        place,
        out_shape=shapes + (jax.ShapeDtypeStruct((1, ROWS), F32),),
        in_specs=[vmem] * 4,
        out_specs=(hbm,) * 3 + (vmem,),
        scratch_shapes=[dma((3,))],
    )(*parts)
    return dq, dk, dv, gr.reshape(ROWS)


def solution(mesh):
    return jax.shard_map(
        body,
        mesh=mesh,
        in_specs=(
            P("seq", "tp"),
            P("seq"),
            P("seq"),
            P("seq", "tp"),
            P("seq", "tp"),
            P("seq", "tp"),
            P("tp", None),
        ),
        out_specs=(P("seq", "tp"), P("seq", "tp"), P("seq", "tp"), P("seq")),
        check_vma=False,
    )
```

```python
import math

import jax
import jax.numpy as jnp
from jax import lax
from jax.experimental import pallas as pl
from jax.experimental.pallas import tpu as pltpu
from jax.sharding import PartitionSpec as P

F32 = jnp.float32
BF = jnp.bfloat16
MESH = pl.DeviceIdType.MESH
NN = ((1,), (0,))
NT = ((1,), (1,))
TN = ((0,), (0,))

HD = 128
GROUP = 8
SEQ = 16
TP = 8
CHIPS = 8
ROWS = 256
HALF = 128
LANES = 2048
WIDE = 1024
FACTOR = 1.0 / math.sqrt(HD)
SCALE = FACTOR * math.log2(math.e)
FLOOR = -1e30


def dot(a, b, dims):
    return lax.dot_general(a, b, (dims, ((), ())), preferred_element_type=F32)


def loop(count, step):
    def run(i, carry):
        step(i)
        return carry

    lax.fori_loop(0, count, run, 0)


def loop_from(first, last, step):
    def run(i, carry):
        step(i)
        return carry

    lax.fori_loop(first, last, run, 0)


def kernel(
    go_hbm,
    w_hbm,
    sel_ref,
    router_ref,
    q_hbm,
    k_hbm,
    v_hbm,
    dq_ref,
    dk_ref,
    dv_ref,
    gr_ref,
    probs,
    w_ref,
    picked,
    keys,
    values,
    acc,
    out_side,
    in_side,
    out_part,
    in_part,
    q_ref,
    q_t,
    q_s,
    top,
    o_t,
    g_t,
    do_t,
    do_s,
    delta,
    dq_t,
    router_part,
    local_sem,
    kv_send,
    kv_recv,
    side_send,
    pick_send,
    pick_recv,
    fold_send,
    fold_recv,
    part_send,
    part_recv,
    router_send,
    router_recv,
):
    s = lax.axis_index("seq")
    t = lax.axis_index("tp")
    chip = s // 2
    core = s % 2
    y = chip // 2
    xl = chip % 2
    z = t // 2
    h = t % 2
    sibling = s + 1 - 2 * core
    z_up = ((z + 1) % 4) * 2 + h
    z_down = ((z + 3) % 4) * 2 + h
    z_far = ((z + 2) % 4) * 2 + h
    x_far = z * 2 + 1 - h
    other = 1 - 2 * h

    def remote(src, dst, send, recv, to):
        return pltpu.make_async_remote_copy(
            src_ref=src,
            dst_ref=dst,
            send_sem=send,
            recv_sem=recv,
            device_id=to,
            device_id_type=MESH,
        )

    mine = pl.ds(pl.multiple_of(core * ROWS, ROWS), ROWS)
    theirs = pl.ds(pl.multiple_of((1 - core) * ROWS, ROWS), ROWS)
    kv_inputs = [
        pltpu.make_async_copy(k_hbm, keys.at[chip, mine, :], local_sem.at[5]),
        pltpu.make_async_copy(v_hbm, values.at[chip, mine, :], local_sem.at[6]),
    ]
    for copy in kv_inputs:
        copy.start()
    go_copies = []
    for p in range(4):
        go_copies.append(
            pltpu.make_async_copy(
                go_hbm.at[pl.ds(p * 512, 512), :],
                probs.at[p // 2, :, pl.ds((p % 2) * WIDE, WIDE)],
                local_sem.at[p],
            )
        )
    for copy in go_copies:
        copy.start()
    w_copy = pltpu.make_async_copy(w_hbm, w_ref, local_sem.at[4])
    q_copy = pltpu.make_async_copy(q_hbm, q_ref, local_sem.at[7])
    q_copy.start()

    barrier = pltpu.get_barrier_semaphore()
    pl.semaphore_signal(barrier, inc=1, device_id=(sibling, t), device_id_type=MESH)
    for step in range(1, CHIPS):
        pl.semaphore_signal(
            barrier,
            inc=1,
            device_id=(((chip + step) % CHIPS) * 2 + core, t),
            device_id_type=MESH,
        )
    for step in range(1, TP):
        pl.semaphore_signal(
            barrier, inc=1, device_id=(s, (t + step) % TP), device_id_type=MESH
        )

    def choose(c):
        sel_half = jnp.transpose(
            jnp.broadcast_to(sel_ref[0:1, c * HALF : (c + 1) * HALF], (HALF, HALF))
        )
        total = jnp.zeros((HALF, WIDE), F32)
        for p in range(4):
            if c == 0:
                go_copies[p].wait()
            pieces = []
            for b in range(4):
                token = lax.broadcasted_iota(jnp.int32, (HALF, HALF), 1) + (p * 512 + b * 128)
                pieces.append(jnp.where(token == sel_half, 1.0, 0.0).astype(BF))
            chosen = jnp.concatenate(pieces, axis=1)
            total += dot(chosen, probs[p // 2, :, (p % 2) * WIDE : (p % 2 + 1) * WIDE], NN)
        picked[t, c * HALF : (c + 1) * HALF, :] = total.astype(BF)

    choose(0)
    for copy in kv_inputs:
        copy.wait()
    pl.semaphore_wait(barrier, CHIPS + TP - 1)

    def block_of(i, block):
        rows = pl.ds(pl.multiple_of((block % 2) * ROWS, ROWS), ROWS)
        return (keys, values)[i].at[block // 2, rows, :]

    def kv_copy(i, n, block, to):
        part = block_of(i, block)
        return remote(part, part, kv_send.at[i, n], kv_recv.at[i, block], (to, t))

    def later_chips(i, act):
        for step in range(1, CHIPS):

            @pl.when(chip + step < CHIPS)
            def _(step=step):
                act(kv_copy(i, step, s, (chip + step) * 2 + core))

    def side_copy(i, d):
        block = (chip - d) * 2 + core
        part = block_of(i, block)
        return remote(part, part, side_send.at[i, d], kv_recv.at[i, block], (sibling, t))

    def kv_ahead(i, d):
        @pl.when(d <= chip)
        def _():
            kv_copy(i, 0, (chip - d) * 2 + core, sibling).wait_recv()
            side_copy(i, d).start()

    def kv_arrived(i, d):
        kv_copy(i, 0, (chip - d) * 2 + 1 - core, sibling).wait_recv()

    def start_all(copies):
        for copy in copies:
            copy.start()

    def arrive_all(copies):
        for copy in copies:
            copy.wait_recv()

    side_copy(0, 0).start()
    later_chips(0, lambda copy: copy.start())
    side_copy(1, 0).start()

    def pick_copy(c, n, slot, to, at=0, rows=HALF):
        src = picked.at[slot, pl.ds(c * HALF + at, rows), :]
        return remote(src, src, pick_send.at[c, n], pick_recv.at[c, n], (s, to))

    quarter = HALF // 2

    def own_sends(c):
        return [
            pick_copy(c, 2, t, x_far),
            pick_copy(c, 0, t, z_up),
            pick_copy(c, 1, t, z_down),
        ]

    def half_sends(c):
        return [
            pick_copy(c, 3, z_down, z_up, 0, quarter),
            pick_copy(c, 4, z_up, z_down, quarter, quarter),
        ]

    def cross_sends(c):
        return [pick_copy(c, 5, x_far, z_up), pick_copy(c, 6, x_far, z_down)]

    def far_sends(c):
        return [pick_copy(c, 7, z_far, x_far)]

    def near_arrivals(c):
        return [pick_copy(c, 0, z_down, z_up), pick_copy(c, 1, z_up, z_down)]

    def x_arrivals(c):
        return [pick_copy(c, 2, x_far, x_far)]

    def half_arrivals(c):
        return [
            pick_copy(c, 3, z_far, z_up, 0, quarter),
            pick_copy(c, 4, z_far, z_down, quarter, quarter),
        ]

    def cross_arrivals(c):
        return [
            pick_copy(c, 5, z_down + other, z_up),
            pick_copy(c, 6, z_up + other, z_down),
        ]

    def far_arrivals(c):
        return [pick_copy(c, 7, z_far + other, x_far)]

    start_all(own_sends(0))
    choose(1)
    w_copy.start()
    later_chips(1, lambda copy: copy.start())

    q_copy.wait()
    for n in range(GROUP):
        block = q_ref[:, n * HD : (n + 1) * HD]
        q_s[n * ROWS : (n + 1) * ROWS, :] = block
        q_t[:, n * ROWS : (n + 1) * ROWS] = jnp.transpose(block)

    def hidden(k):
        key_at = lax.broadcasted_iota(jnp.int32, (512, LANES), 0) + k * 512
        row_at = (lax.broadcasted_iota(jnp.int32, (512, LANES), 1) % ROWS) + s * ROWS
        return key_at > row_at

    top[...] = jnp.full_like(top, FLOOR)

    def first_pass(k, masked):
        scores = dot(keys[k], q_t[...], NN)
        if masked:
            scores = jnp.where(hidden(k), FLOOR, scores)
        top[...] = jnp.maximum(top[...], jnp.max(scores.reshape(64, 8, LANES), axis=0))

    def first_step(d):
        kv_ahead(0, d + 1)

        @pl.when(d <= chip)
        def _():
            kv_arrived(0, d)
            first_pass(chip - d, False)

        @pl.when(d == 2)
        def _():
            arrive_all(near_arrivals(0))
            start_all(half_sends(0))

    start_all(own_sends(1))
    kv_arrived(0, 0)
    first_pass(chip, True)
    kv_ahead(0, 1)
    loop_from(1, CHIPS, first_step)
    kv_ahead(1, 1)

    peak = jnp.max(top[...], axis=0, keepdims=True) * SCALE
    top[...] = jnp.broadcast_to(peak, top.shape)
    o_t[...] = jnp.zeros_like(o_t)

    def second_pass(k, masked):
        values_t = jnp.concatenate(
            [jnp.transpose(values[k]), jnp.ones((16, 512), BF)], axis=0
        )
        scores = dot(keys[k], q_t[...], NN) * SCALE - top[0:1, :]
        if masked:
            scores = jnp.where(hidden(k), FLOOR, scores)
        weights = jnp.exp2(scores).astype(BF)
        probs[k] = weights
        o_t[...] += dot(values_t, weights, NN)

    def second_step(d):
        kv_ahead(1, d + 1)

        @pl.when(d <= chip)
        def _():
            kv_arrived(1, d)
            second_pass(chip - d, False)

        @pl.when(d == 1)
        def _():
            arrive_all(half_arrivals(0))
            start_all(far_sends(0))

        @pl.when(d == 2)
        def _():
            arrive_all(half_arrivals(1))
            start_all(far_sends(1))

    arrive_all(near_arrivals(1))
    start_all(half_sends(1))
    for c in range(2):
        arrive_all(x_arrivals(c))
        start_all(cross_sends(c))
    kv_arrived(1, 0)
    second_pass(chip, True)
    loop_from(1, CHIPS, second_step)

    def project(slot, fresh=False):
        columns = pl.ds(pl.multiple_of(slot * WIDE, WIDE), WIDE)
        term = dot(w_ref[:, columns], picked[slot], NT)
        if fresh:
            g_t[...] = term
        else:
            g_t[...] += term

    w_copy.wait()
    project(t, True)
    project(z_down)
    project(z_up)
    project(x_far)
    project(z_far)
    arrive_all(cross_arrivals(0) + cross_arrivals(1))
    project(z_down + other)
    project(z_up + other)
    arrive_all(far_arrivals(0) + far_arrivals(1))
    project(z_far + other)

    router_row = router_ref[...]
    router_sum = jnp.zeros((1, ROWS), F32)
    for n in range(GROUP):
        lanes = slice(n * ROWS, (n + 1) * ROWS)
        g = g_t[n * HD : (n + 1) * HD, :]
        inverse = 1.0 / o_t[HD : HD + 1, lanes]
        share = jnp.sum(g * o_t[0:HD, lanes], axis=0, keepdims=True) * inverse
        router_sum += share
        level = router_row * inverse
        delta[0:1, lanes] = share * level
        scaled = g * level
        do_t[:, lanes] = scaled.astype(BF)
        do_s[lanes, :] = jnp.transpose(scaled).astype(BF)
    router_part[t] = jnp.broadcast_to(router_sum, (8, ROWS))

    def router_copy(step, slot):
        part = router_part.at[slot]
        return remote(
            part, part, router_send.at[step], router_recv.at[slot], (s, (t + step) % TP)
        )

    for step in range(1, TP):
        router_copy(step, t).start()

    def fold_copy(k):
        return remote(
            out_side.at[k], in_side.at[k], fold_send.at[k], fold_recv.at[k], (sibling, t)
        )

    def part_copy(k, source):
        return remote(
            out_part.at[k],
            in_part.at[source],
            part_send.at[k],
            part_recv.at[source],
            (k * 2 + core, t),
        )

    def backward_step(k):
        weights = probs[k]
        grad_probs = dot(values[k], do_t[...], NN) - delta[0:1, :]
        grad_scores = (weights.astype(F32) * grad_probs).astype(BF)
        acc[k, 1] = dot(weights, do_s[...], NN)
        acc[k, 0] = dot(grad_scores, q_s[...], NN)
        probs[k] = grad_scores
        for n in range(2):
            out_side[k, n] = acc[k, n, theirs, :].astype(BF)
        fold_copy(k).start()

    def fold(k):
        fold_copy(k).wait_recv()
        for n in range(2):
            acc[k, n, mine, :] += in_side[k, n].astype(F32)

    def pass_on(k):
        fold(k)
        for n in range(2):
            out_part[k, n] = acc[k, n, mine, :].astype(BF)
        part_copy(k, chip).start()

    def turn(i):
        after = (i + 4) // 6
        to_y = (1 - after) + after * 2 * ((i + 1) % 2)
        across = (1 - after) * (1 - i % 2) + after * (1 - i // 4)
        ordered = to_y * 2 + (xl + across) % 2
        last = i // 6
        return (y // 3) * ((1 - last) * ordered + last * i) + (1 - y // 3) * i

    def backward(i):
        backward_step(turn(i))

        @pl.when(i > 0)
        def _():
            pass_on(turn(i - 1))

    loop(chip + 1, backward)

    dq_t[...] = jnp.zeros_like(dq_t)

    def query_step(k):
        dq_t[...] += dot(keys[k], probs[k], TN)

    loop(chip + 1, query_step)
    for n in range(GROUP):
        block = jnp.transpose(dq_t[:, n * ROWS : (n + 1) * ROWS]) * FACTOR
        dq_ref[:, n * HD : (n + 1) * HD] = block.astype(BF)

    router_total = router_part[t]
    for step in range(1, TP):
        slot = (t + step) % TP
        router_copy(step, slot).wait_recv()
        router_total += router_part[slot]
    gr_ref[...] = router_total

    fold(chip)

    def collect(source):
        @pl.when(source > chip)
        def _():
            part_copy(chip, source).wait_recv()
            for i in range(2):
                acc[chip, i, mine, :] += in_part[source, i].astype(F32)

    loop(CHIPS, collect)
    dk_ref[...] = (acc[chip, 0, mine, :] * FACTOR).astype(BF)
    dv_ref[...] = acc[chip, 1, mine, :].astype(BF)

    for i in range(2):
        later_chips(i, lambda copy: copy.wait_send())
    for c in range(2):
        for copy in own_sends(c) + half_sends(c) + cross_sends(c) + far_sends(c):
            copy.wait_send()
    for step in range(1, TP):
        router_copy(step, t).wait_send()

    def sent(k):
        @pl.when(k <= chip)
        def _():
            side_copy(0, k).wait_send()
            side_copy(1, k).wait_send()
            fold_copy(k).wait_send()

        @pl.when(k < chip)
        def _():
            part_copy(k, chip).wait_send()

    loop(CHIPS, sent)


def place(dq_in, dk_in, dv_in, gr_in, dq_ref, dk_ref, dv_ref, gr_ref, sem):
    copies = [
        pltpu.make_async_copy(dq_in, dq_ref, sem.at[0]),
        pltpu.make_async_copy(dk_in, dk_ref, sem.at[1]),
        pltpu.make_async_copy(dv_in, dv_ref, sem.at[2]),
    ]
    for copy in copies:
        copy.start()
    gr_ref[...] = gr_in[0:1, :]
    for copy in copies:
        copy.wait()


def body(grad_out, select, router, query, key_rows, value_rows, out_weight):
    vmem = pl.BlockSpec(memory_space=pltpu.VMEM)
    hbm = pl.BlockSpec(memory_space=pl.ANY)
    dma = pltpu.SemaphoreType.DMA
    shapes = (
        jax.ShapeDtypeStruct((ROWS, WIDE), BF),
        jax.ShapeDtypeStruct((ROWS, HD), BF),
        jax.ShapeDtypeStruct((ROWS, HD), BF),
    )
    parts = pl.pallas_call(
        kernel,
        out_shape=shapes + (jax.ShapeDtypeStruct((8, ROWS), F32),),
        in_specs=[hbm, hbm, vmem, vmem, hbm, hbm, hbm],
        out_specs=(vmem,) * 4,
        scratch_shapes=[
            pltpu.VMEM((CHIPS, 512, LANES), BF),
            pltpu.VMEM((WIDE, TP * WIDE), BF),
            pltpu.VMEM((TP, ROWS, WIDE), BF),
            pltpu.VMEM((CHIPS, 512, HD), BF),
            pltpu.VMEM((CHIPS, 512, HD), BF),
            pltpu.VMEM((CHIPS, 2, 512, HD), F32),
            pltpu.VMEM((CHIPS, 2, ROWS, HD), BF),
            pltpu.VMEM((CHIPS, 2, ROWS, HD), BF),
            pltpu.VMEM((CHIPS, 2, ROWS, HD), BF),
            pltpu.VMEM((CHIPS, 2, ROWS, HD), BF),
            pltpu.VMEM((ROWS, WIDE), BF),
            pltpu.VMEM((HD, LANES), BF),
            pltpu.VMEM((LANES, HD), BF),
            pltpu.VMEM((8, LANES), F32),
            pltpu.VMEM((HD + 16, LANES), F32),
            pltpu.VMEM((WIDE, ROWS), F32),
            pltpu.VMEM((HD, LANES), BF),
            pltpu.VMEM((LANES, HD), BF),
            pltpu.VMEM((8, LANES), F32),
            pltpu.VMEM((HD, LANES), F32),
            pltpu.VMEM((TP, 8, ROWS), F32),
            dma((8,)),
            dma((2, CHIPS)),
            dma((2, SEQ)),
            dma((2, CHIPS)),
            dma((2, 8)),
            dma((2, 8)),
            dma((CHIPS,)),
            dma((CHIPS,)),
            dma((CHIPS,)),
            dma((CHIPS,)),
            dma((TP,)),
            dma((TP,)),
        ],
        compiler_params=pltpu.CompilerParams(
            collective_id=0, has_side_effects=True, vmem_limit_bytes=62 << 20
        ),
    )(
        grad_out,
        out_weight,
        select.reshape(1, ROWS),
        router.reshape(1, ROWS),
        query,
        key_rows,
        value_rows,
    )
    dq, dk, dv, gr = pl.pallas_call(
        place,
        out_shape=shapes + (jax.ShapeDtypeStruct((1, ROWS), F32),),
        in_specs=[vmem] * 4,
        out_specs=(hbm,) * 3 + (vmem,),
        scratch_shapes=[dma((3,))],
    )(*parts)
    return dq, dk, dv, gr.reshape(ROWS)


def solution(mesh):
    return jax.shard_map(
        body,
        mesh=mesh,
        in_specs=(
            P("seq", "tp"),
            P("seq"),
            P("seq"),
            P("seq", "tp"),
            P("seq", "tp"),
            P("seq", "tp"),
            P("tp", None),
        ),
        out_specs=(P("seq", "tp"), P("seq", "tp"), P("seq", "tp"), P("seq")),
        check_vma=False,
    )
```

```python
import math

import jax
import jax.numpy as jnp
from jax import lax
from jax.experimental import pallas as pl
from jax.experimental.pallas import tpu as pltpu
from jax.sharding import PartitionSpec as P

F32 = jnp.float32
BF = jnp.bfloat16
MESH = pl.DeviceIdType.MESH
NN = ((1,), (0,))
NT = ((1,), (1,))
TN = ((0,), (0,))

HD = 128
GROUP = 8
SEQ = 16
TP = 8
CHIPS = 8
ROWS = 256
HALF = 128
LANES = 2048
WIDE = 1024
FACTOR = 1.0 / math.sqrt(HD)
SCALE = FACTOR * math.log2(math.e)
FLOOR = -1e30


def dot(a, b, dims):
    return lax.dot_general(a, b, (dims, ((), ())), preferred_element_type=F32)


def loop(count, step):
    def run(i, carry):
        step(i)
        return carry

    lax.fori_loop(0, count, run, 0)


def loop_from(first, last, step):
    def run(i, carry):
        step(i)
        return carry

    lax.fori_loop(first, last, run, 0)


def kernel(
    go_hbm,
    w_hbm,
    sel_ref,
    router_ref,
    q_hbm,
    k_hbm,
    v_hbm,
    dq_ref,
    dk_ref,
    dv_ref,
    gr_ref,
    probs,
    w_ref,
    picked,
    keys,
    values,
    acc,
    out_side,
    in_side,
    out_part,
    in_part,
    q_ref,
    q_t,
    q_s,
    top,
    o_t,
    g_t,
    do_t,
    do_s,
    delta,
    dq_t,
    router_part,
    local_sem,
    kv_send,
    kv_recv,
    side_send,
    pick_send,
    pick_recv,
    fold_send,
    fold_recv,
    part_send,
    part_recv,
    router_send,
    router_recv,
):
    s = lax.axis_index("seq")
    t = lax.axis_index("tp")
    chip = s // 2
    core = s % 2
    y = chip // 2
    xl = chip % 2
    z = t // 2
    h = t % 2
    sibling = s + 1 - 2 * core
    z_up = ((z + 1) % 4) * 2 + h
    z_down = ((z + 3) % 4) * 2 + h
    z_far = ((z + 2) % 4) * 2 + h
    x_far = z * 2 + 1 - h
    other = 1 - 2 * h

    def remote(src, dst, send, recv, to):
        return pltpu.make_async_remote_copy(
            src_ref=src,
            dst_ref=dst,
            send_sem=send,
            recv_sem=recv,
            device_id=to,
            device_id_type=MESH,
        )

    mine = pl.ds(pl.multiple_of(core * ROWS, ROWS), ROWS)
    theirs = pl.ds(pl.multiple_of((1 - core) * ROWS, ROWS), ROWS)
    kv_inputs = [
        pltpu.make_async_copy(k_hbm, keys.at[chip, mine, :], local_sem.at[5]),
        pltpu.make_async_copy(v_hbm, values.at[chip, mine, :], local_sem.at[6]),
    ]
    for copy in kv_inputs:
        copy.start()
    go_copies = []
    for p in range(4):
        go_copies.append(
            pltpu.make_async_copy(
                go_hbm.at[pl.ds(p * 512, 512), :],
                probs.at[p // 2, :, pl.ds((p % 2) * WIDE, WIDE)],
                local_sem.at[p],
            )
        )
    for copy in go_copies:
        copy.start()
    w_copy = pltpu.make_async_copy(w_hbm, w_ref, local_sem.at[4])
    q_copy = pltpu.make_async_copy(q_hbm, q_ref, local_sem.at[7])
    q_copy.start()

    barrier = pltpu.get_barrier_semaphore()
    pl.semaphore_signal(barrier, inc=1, device_id=(sibling, t), device_id_type=MESH)
    for step in range(1, CHIPS):
        pl.semaphore_signal(
            barrier,
            inc=1,
            device_id=(((chip + step) % CHIPS) * 2 + core, t),
            device_id_type=MESH,
        )
    for step in range(1, TP):
        pl.semaphore_signal(
            barrier, inc=1, device_id=(s, (t + step) % TP), device_id_type=MESH
        )

    def choose(c):
        sel_half = jnp.transpose(
            jnp.broadcast_to(sel_ref[0:1, c * HALF : (c + 1) * HALF], (HALF, HALF))
        )
        total = jnp.zeros((HALF, WIDE), F32)
        for p in range(4):
            if c == 0:
                go_copies[p].wait()
            pieces = []
            for b in range(4):
                token = lax.broadcasted_iota(jnp.int32, (HALF, HALF), 1) + (p * 512 + b * 128)
                pieces.append(jnp.where(token == sel_half, 1.0, 0.0).astype(BF))
            chosen = jnp.concatenate(pieces, axis=1)
            total += dot(chosen, probs[p // 2, :, (p % 2) * WIDE : (p % 2 + 1) * WIDE], NN)
        picked[t, c * HALF : (c + 1) * HALF, :] = total.astype(BF)

    choose(0)
    for copy in kv_inputs:
        copy.wait()
    pl.semaphore_wait(barrier, CHIPS + TP - 1)

    def block_of(i, block):
        rows = pl.ds(pl.multiple_of((block % 2) * ROWS, ROWS), ROWS)
        return (keys, values)[i].at[block // 2, rows, :]

    def kv_copy(i, n, block, to):
        part = block_of(i, block)
        return remote(part, part, kv_send.at[i, n], kv_recv.at[i, block], (to, t))

    def later_chips(i, act):
        for step in range(1, CHIPS):

            @pl.when(chip + step < CHIPS)
            def _(step=step):
                act(kv_copy(i, step, s, (chip + step) * 2 + core))

    def side_copy(i, d):
        block = (chip - d) * 2 + core
        part = block_of(i, block)
        return remote(part, part, side_send.at[i, d], kv_recv.at[i, block], (sibling, t))

    def kv_ahead(i, d):
        @pl.when(d <= chip)
        def _():
            kv_copy(i, 0, (chip - d) * 2 + core, sibling).wait_recv()
            side_copy(i, d).start()

    def kv_arrived(i, d):
        kv_copy(i, 0, (chip - d) * 2 + 1 - core, sibling).wait_recv()

    def start_all(copies):
        for copy in copies:
            copy.start()

    def arrive_all(copies):
        for copy in copies:
            copy.wait_recv()

    side_copy(0, 0).start()
    later_chips(0, lambda copy: copy.start())
    side_copy(1, 0).start()

    def pick_copy(c, n, slot, to, at=0, rows=HALF):
        src = picked.at[slot, pl.ds(c * HALF + at, rows), :]
        return remote(src, src, pick_send.at[c, n], pick_recv.at[c, n], (s, to))

    quarter = HALF // 2

    def own_sends(c):
        return [
            pick_copy(c, 2, t, x_far),
            pick_copy(c, 0, t, z_up),
            pick_copy(c, 1, t, z_down),
        ]

    def half_sends(c):
        return [
            pick_copy(c, 3, z_down, z_up, 0, quarter),
            pick_copy(c, 4, z_up, z_down, quarter, quarter),
        ]

    def cross_sends(c):
        return [pick_copy(c, 5, x_far, z_up), pick_copy(c, 6, x_far, z_down)]

    def far_sends(c):
        return [pick_copy(c, 7, z_far, x_far)]

    def near_arrivals(c):
        return [pick_copy(c, 0, z_down, z_up), pick_copy(c, 1, z_up, z_down)]

    def x_arrivals(c):
        return [pick_copy(c, 2, x_far, x_far)]

    def half_arrivals(c):
        return [
            pick_copy(c, 3, z_far, z_up, 0, quarter),
            pick_copy(c, 4, z_far, z_down, quarter, quarter),
        ]

    def cross_arrivals(c):
        return [
            pick_copy(c, 5, z_down + other, z_up),
            pick_copy(c, 6, z_up + other, z_down),
        ]

    def far_arrivals(c):
        return [pick_copy(c, 7, z_far + other, x_far)]

    start_all(own_sends(0))
    choose(1)
    w_copy.start()
    later_chips(1, lambda copy: copy.start())

    q_copy.wait()
    for n in range(GROUP):
        block = q_ref[:, n * HD : (n + 1) * HD]
        q_s[n * ROWS : (n + 1) * ROWS, :] = block
        q_t[:, n * ROWS : (n + 1) * ROWS] = jnp.transpose(block)

    def hidden(k):
        key_at = lax.broadcasted_iota(jnp.int32, (512, LANES), 0) + k * 512
        row_at = (lax.broadcasted_iota(jnp.int32, (512, LANES), 1) % ROWS) + s * ROWS
        return key_at > row_at

    top[...] = jnp.full_like(top, FLOOR)

    def first_pass(k, masked):
        scores = dot(keys[k], q_t[...], NN)
        if masked:
            scores = jnp.where(hidden(k), FLOOR, scores)
        top[...] = jnp.maximum(top[...], jnp.max(scores.reshape(64, 8, LANES), axis=0))

    def first_step(d):
        kv_ahead(0, d + 1)

        @pl.when(d <= chip)
        def _():
            kv_arrived(0, d)
            first_pass(chip - d, False)

        @pl.when(d == 2)
        def _():
            arrive_all(near_arrivals(0))
            start_all(half_sends(0))

    start_all(own_sends(1))
    kv_arrived(0, 0)
    first_pass(chip, True)
    kv_ahead(0, 1)
    loop_from(1, CHIPS, first_step)
    kv_ahead(1, 1)

    peak = jnp.max(top[...], axis=0, keepdims=True) * SCALE
    top[...] = jnp.broadcast_to(peak, top.shape)
    o_t[...] = jnp.zeros_like(o_t)

    def second_pass(k, masked):
        values_t = jnp.concatenate(
            [jnp.transpose(values[k]), jnp.ones((16, 512), BF)], axis=0
        )
        scores = dot(keys[k], q_t[...], NN) * SCALE - top[0:1, :]
        if masked:
            scores = jnp.where(hidden(k), FLOOR, scores)
        weights = jnp.exp2(scores).astype(BF)
        probs[k] = weights
        o_t[...] += dot(values_t, weights, NN)

    def second_step(d):
        kv_ahead(1, d + 1)

        @pl.when(d <= chip)
        def _():
            kv_arrived(1, d)
            second_pass(chip - d, False)

        @pl.when(d == 1)
        def _():
            arrive_all(half_arrivals(0))
            start_all(far_sends(0))

        @pl.when(d == 2)
        def _():
            arrive_all(half_arrivals(1))
            start_all(far_sends(1))

    arrive_all(near_arrivals(1))
    start_all(half_sends(1))
    for c in range(2):
        arrive_all(x_arrivals(c))
        start_all(cross_sends(c))
    kv_arrived(1, 0)
    second_pass(chip, True)
    loop_from(1, CHIPS, second_step)

    def project(slot, fresh=False):
        columns = pl.ds(pl.multiple_of(slot * WIDE, WIDE), WIDE)
        term = dot(w_ref[:, columns], picked[slot], NT)
        if fresh:
            g_t[...] = term
        else:
            g_t[...] += term

    w_copy.wait()
    project(t, True)
    project(z_down)
    project(z_up)
    project(x_far)
    project(z_far)
    arrive_all(cross_arrivals(0) + cross_arrivals(1))
    project(z_down + other)
    project(z_up + other)
    arrive_all(far_arrivals(0) + far_arrivals(1))
    project(z_far + other)

    router_row = router_ref[...]
    router_sum = jnp.zeros((1, ROWS), F32)
    for n in range(GROUP):
        lanes = slice(n * ROWS, (n + 1) * ROWS)
        g = g_t[n * HD : (n + 1) * HD, :]
        inverse = 1.0 / o_t[HD : HD + 1, lanes]
        share = jnp.sum(g * o_t[0:HD, lanes], axis=0, keepdims=True) * inverse
        router_sum += share
        level = router_row * inverse
        delta[0:1, lanes] = share * level
        scaled = (g * level).astype(BF)
        do_t[:, lanes] = scaled
        do_s[lanes, :] = jnp.transpose(scaled)
    router_part[t] = jnp.broadcast_to(router_sum, (8, ROWS))

    def router_copy(step, slot):
        part = router_part.at[slot]
        return remote(
            part, part, router_send.at[step], router_recv.at[slot], (s, (t + step) % TP)
        )

    for step in range(1, TP):
        router_copy(step, t).start()

    def fold_copy(k):
        return remote(
            out_side.at[k], in_side.at[k], fold_send.at[k], fold_recv.at[k], (sibling, t)
        )

    def part_copy(k, source):
        return remote(
            out_part.at[k],
            in_part.at[source],
            part_send.at[k],
            part_recv.at[source],
            (k * 2 + core, t),
        )

    def backward_step(k):
        weights = probs[k]
        grad_probs = dot(values[k], do_t[...], NN) - delta[0:1, :]
        grad_scores = (weights.astype(F32) * grad_probs).astype(BF)
        acc[k, 1] = dot(weights, do_s[...], NN)
        acc[k, 0] = dot(grad_scores, q_s[...], NN)
        probs[k] = grad_scores
        for n in range(2):
            out_side[k, n] = acc[k, n, theirs, :].astype(BF)
        fold_copy(k).start()

    def fold(k):
        fold_copy(k).wait_recv()
        for n in range(2):
            acc[k, n, mine, :] += in_side[k, n].astype(F32)

    def pass_on(k):
        fold(k)
        for n in range(2):
            out_part[k, n] = acc[k, n, mine, :].astype(BF)
        part_copy(k, chip).start()

    def turn(i):
        after = (i + 4) // 6
        to_y = (1 - after) + after * 2 * ((i + 1) % 2)
        across = (1 - after) * (1 - i % 2) + after * (1 - i // 4)
        ordered = to_y * 2 + (xl + across) % 2
        last = i // 6
        return (y // 3) * ((1 - last) * ordered + last * i) + (1 - y // 3) * i

    def backward(i):
        backward_step(turn(i))

        @pl.when(i > 0)
        def _():
            pass_on(turn(i - 1))

    loop(chip + 1, backward)

    dq_t[...] = jnp.zeros_like(dq_t)

    def query_step(k):
        dq_t[...] += dot(keys[k], probs[k], TN)

    loop(chip + 1, query_step)
    for n in range(GROUP):
        block = (dq_t[:, n * ROWS : (n + 1) * ROWS] * FACTOR).astype(BF)
        dq_ref[:, n * HD : (n + 1) * HD] = jnp.transpose(block)

    router_total = router_part[t]
    for step in range(1, TP):
        slot = (t + step) % TP
        router_copy(step, slot).wait_recv()
        router_total += router_part[slot]
    gr_ref[...] = router_total

    fold(chip)

    def collect(source):
        @pl.when(source > chip)
        def _():
            part_copy(chip, source).wait_recv()
            for i in range(2):
                acc[chip, i, mine, :] += in_part[source, i].astype(F32)

    loop(CHIPS, collect)
    dk_ref[...] = (acc[chip, 0, mine, :] * FACTOR).astype(BF)
    dv_ref[...] = acc[chip, 1, mine, :].astype(BF)

    for i in range(2):
        later_chips(i, lambda copy: copy.wait_send())
    for c in range(2):
        for copy in own_sends(c) + half_sends(c) + cross_sends(c) + far_sends(c):
            copy.wait_send()
    for step in range(1, TP):
        router_copy(step, t).wait_send()

    def sent(k):
        @pl.when(k <= chip)
        def _():
            side_copy(0, k).wait_send()
            side_copy(1, k).wait_send()
            fold_copy(k).wait_send()

        @pl.when(k < chip)
        def _():
            part_copy(k, chip).wait_send()

    loop(CHIPS, sent)


def place(dq_in, dk_in, dv_in, gr_in, dq_ref, dk_ref, dv_ref, gr_ref, sem):
    copies = [
        pltpu.make_async_copy(dq_in, dq_ref, sem.at[0]),
        pltpu.make_async_copy(dk_in, dk_ref, sem.at[1]),
        pltpu.make_async_copy(dv_in, dv_ref, sem.at[2]),
    ]
    for copy in copies:
        copy.start()
    gr_ref[...] = gr_in[0:1, :]
    for copy in copies:
        copy.wait()


def body(grad_out, select, router, query, key_rows, value_rows, out_weight):
    vmem = pl.BlockSpec(memory_space=pltpu.VMEM)
    hbm = pl.BlockSpec(memory_space=pl.ANY)
    dma = pltpu.SemaphoreType.DMA
    shapes = (
        jax.ShapeDtypeStruct((ROWS, WIDE), BF),
        jax.ShapeDtypeStruct((ROWS, HD), BF),
        jax.ShapeDtypeStruct((ROWS, HD), BF),
    )
    parts = pl.pallas_call(
        kernel,
        out_shape=shapes + (jax.ShapeDtypeStruct((8, ROWS), F32),),
        in_specs=[hbm, hbm, vmem, vmem, hbm, hbm, hbm],
        out_specs=(vmem,) * 4,
        scratch_shapes=[
            pltpu.VMEM((CHIPS, 512, LANES), BF),
            pltpu.VMEM((WIDE, TP * WIDE), BF),
            pltpu.VMEM((TP, ROWS, WIDE), BF),
            pltpu.VMEM((CHIPS, 512, HD), BF),
            pltpu.VMEM((CHIPS, 512, HD), BF),
            pltpu.VMEM((CHIPS, 2, 512, HD), F32),
            pltpu.VMEM((CHIPS, 2, ROWS, HD), BF),
            pltpu.VMEM((CHIPS, 2, ROWS, HD), BF),
            pltpu.VMEM((CHIPS, 2, ROWS, HD), BF),
            pltpu.VMEM((CHIPS, 2, ROWS, HD), BF),
            pltpu.VMEM((ROWS, WIDE), BF),
            pltpu.VMEM((HD, LANES), BF),
            pltpu.VMEM((LANES, HD), BF),
            pltpu.VMEM((8, LANES), F32),
            pltpu.VMEM((HD + 16, LANES), F32),
            pltpu.VMEM((WIDE, ROWS), F32),
            pltpu.VMEM((HD, LANES), BF),
            pltpu.VMEM((LANES, HD), BF),
            pltpu.VMEM((8, LANES), F32),
            pltpu.VMEM((HD, LANES), F32),
            pltpu.VMEM((TP, 8, ROWS), F32),
            dma((8,)),
            dma((2, CHIPS)),
            dma((2, SEQ)),
            dma((2, CHIPS)),
            dma((2, 8)),
            dma((2, 8)),
            dma((CHIPS,)),
            dma((CHIPS,)),
            dma((CHIPS,)),
            dma((CHIPS,)),
            dma((TP,)),
            dma((TP,)),
        ],
        compiler_params=pltpu.CompilerParams(
            collective_id=0, has_side_effects=True, vmem_limit_bytes=62 << 20
        ),
    )(
        grad_out,
        out_weight,
        select.reshape(1, ROWS),
        router.reshape(1, ROWS),
        query,
        key_rows,
        value_rows,
    )
    dq, dk, dv, gr = pl.pallas_call(
        place,
        out_shape=shapes + (jax.ShapeDtypeStruct((1, ROWS), F32),),
        in_specs=[vmem] * 4,
        out_specs=(hbm,) * 3 + (vmem,),
        scratch_shapes=[dma((3,))],
    )(*parts)
    return dq, dk, dv, gr.reshape(ROWS)


def solution(mesh):
    return jax.shard_map(
        body,
        mesh=mesh,
        in_specs=(
            P("seq", "tp"),
            P("seq"),
            P("seq"),
            P("seq", "tp"),
            P("seq", "tp"),
            P("seq", "tp"),
            P("tp", None),
        ),
        out_specs=(P("seq", "tp"), P("seq", "tp"), P("seq", "tp"), P("seq")),
        check_vma=False,
    )
```
